32 devices in a mesh: gx: 4 (over z), gy: 8 (over y, x, core).
Axes of the slice: x: 2, y: 2, z: 4, core: 2. Of those that a mesh axis runs over, the one named last changes fastest.
Arguments:
- velocity: float32 [3, 384, 128, 128], P(None, 'gx', 'gy'), may hold values from -6 to 6
- states: float32 [2, 384, 128, 128], P(None, 'gx', 'gy'), may hold values from -6 to 6
- pull_plan: int32 [24, 8], P('gx', 'gy'), may hold values from 0 to 15, as said below
- send_plan: int32 [4, 8, 8, 2], P('gx', 'gy'), may hold values from -1 to 5, as said below
- codes: int32 [3, 24, 8], P(None, 'gx', 'gy'), may hold values from 0 to 1023, as said below
Outputs:
- hessian_velocity: float32 [3, 384, 128, 128], P(None, 'gx', 'gy')
The draws below stay inside these ranges and needn't reach their ends.
Inputs may be any that keep to these rules, and one draw needn't show every extreme that they name: `pull_plan`: the bricks of one device name distinct slots; slot p of device (g, h) is filled by device (g, p // 2) along gy. Every device uses 2 slots from at least one supplying device, and at most 2 from any. send_plan[g, s, h, e] is the brick of device (g, s), in order of brick rows then brick columns within the device, that fills slot s * 2 + e of device (g, h), or -1 where no brick of device (g, h) names that slot; it agrees with pull_plan. codes[0] and codes[1] lie in 0 .. 7; codes[2] is the depth position in units of 1 / 8 cell.
All inputs are finite; a program needn't handle non-finite values.
Results may differ from the reference program's by a relative error of at most 0.00013.
Values sent between devices are 32-bit elements; how exact they have to be, the bound alone decides.
A program may use at most 128 MiB of HBM per device.

```python
import jax
import jax.numpy as jnp
from jax import lax

CX = 96
CY = 16
CZ = 128
BX = 16
BY = 16
CAP = 2
QF = 8
STEPS = 2
NX = 384
NY = 128
BRX_DEV = 6
BRY_DEV = 1
BRX = 24
BRY = 8
GX_DEVS = 4
GY_DEVS = 8


def plan_tables(key):
    base = jax.random.fold_in(key, 11)
    key_hot, key_noise, key_pairs, key_local, key_order = jax.random.split(base, 5)
    bricks = CX // BX * (CY // BY)
    lowest = max(1, -(-(bricks - GY_DEVS) // (CAP - 1)))
    highest = bricks // CAP
    hotness = jax.random.randint(key_hot, (GX_DEVS, 1, GY_DEVS), 0, 64)
    jitter = jax.random.randint(key_noise, (GX_DEVS, GY_DEVS, GY_DEVS), 0, 32)
    favour = jnp.zeros((GX_DEVS, GY_DEVS, GY_DEVS), jnp.int32).at[:, 0, GY_DEVS - 1].set(1000)
    ranking = (hotness + jitter + favour) * GY_DEVS + jnp.arange(GY_DEVS, dtype=jnp.int32)[None, None, :]
    wanted = bricks - lowest * (CAP - 1)
    _, ranked = lax.top_k(ranking, wanted)
    ranked = ranked.astype(jnp.int32)
    doubled = jax.random.randint(key_pairs, (GX_DEVS, GY_DEVS, 1), lowest, highest + 1)
    brick_order = jnp.arange(bricks, dtype=jnp.int32)[None, None, :]
    grouped = brick_order < CAP * doubled
    position = jnp.where(grouped, brick_order // CAP, brick_order - doubled * (CAP - 1))
    slot_number = jnp.where(grouped, brick_order % CAP, 0)
    supplier = jnp.take_along_axis(ranked, position, axis=2)
    local_brick = jax.random.randint(key_local, (GX_DEVS, GY_DEVS, bricks), 0, bricks)
    local_brick = local_brick.at[0, 0, 0].set(bricks - 1)
    pulled = supplier * CAP + slot_number
    shuffles = jax.vmap(lambda subkey: jax.random.permutation(subkey, bricks))(jax.random.split(key_order, GX_DEVS * GY_DEVS)).reshape(GX_DEVS, GY_DEVS, bricks)
    pulled = jnp.take_along_axis(pulled, shuffles.astype(jnp.int32), axis=2)
    pull_grid = pulled.reshape(GX_DEVS, GY_DEVS, CX // BX, CY // BY).transpose(0, 2, 1, 3)
    pull_grid = pull_grid.reshape(GX_DEVS * (CX // BX), GY_DEVS * (CY // BY))
    matches = (supplier[:, None, :, None, :] == jnp.arange(GY_DEVS, dtype=jnp.int32)[None, :, None, None, None]) & (slot_number[:, None, :, None, :] == jnp.arange(CAP, dtype=jnp.int32)[None, None, None, :, None])
    sending = jnp.sum(jnp.where(matches, local_brick[:, None, :, None, :] + 1, 0), axis=4) - 1
    return (pull_grid.astype(jnp.int32), sending.astype(jnp.int32))


def draw_pull_plan(key, part):
    return plan_tables(key)[0]


def draw_send_plan(key, part):
    return plan_tables(key)[1]


def draw_codes(key, part):
    base = jax.random.fold_in(key, 23)
    key_fine, key_depth = jax.random.split(base, 2)
    fine = jax.random.randint(key_fine, (2, BRX, BRY), 0, QF)
    fine = fine.at[1, 0, 0].set(0)
    deep = jax.random.randint(key_depth, (1, BRX, BRY), 0, CZ * QF)
    deep = deep.at[0, 0, 0].set(CZ * QF - 1)
    return jnp.concatenate([fine, deep], axis=0).astype(jnp.int32)


def block_scale(stream_key, shape, pieces, smallest, top_value):
    def one(dim, blocks):
        draws = jax.random.uniform(jax.random.fold_in(jax.random.fold_in(stream_key, 6), dim), (blocks,), jnp.float32, smallest / len(pieces), top_value / len(pieces))
        return jnp.repeat(jnp.exp(draws), shape[dim] // blocks).reshape((-1,) + (1,) * (len(shape) - dim - 1))

    gain = one(*pieces[0])
    for cut in pieces[1:]:
        gain = gain * one(*cut)
    return gain


def noise(rng, shape, deviation, reach, cuts=(), kind=jnp.bfloat16):
    drawn = jax.random.normal(rng, shape, jnp.float32) * deviation
    if len(cuts) > 0:
        drawn = block_scale(rng, shape, cuts, -0.22, 0.18) * drawn
    return jnp.clip(drawn, min=-reach, max=reach).astype(kind)


def setup_inputs(seed: int = 0) -> dict:
    key_list = jax.random.split(jax.random.key(seed), 6)
    return {
        "velocity": noise(key_list[0], (3, NX, NY, CZ), 1.0, 6.0, ((1, 4), (2, 8)), jnp.float32),
        "states": noise(key_list[1], (STEPS, NX, NY, CZ), 1.0, 6.0, ((1, 4), (2, 8)), jnp.float32),
        "pull_plan": draw_pull_plan(jax.random.fold_in(key_list[5], 71), 0),
        "send_plan": draw_send_plan(jax.random.fold_in(key_list[5], 71), 0),
        "codes": draw_codes(jax.random.fold_in(key_list[5], 71), 0),
    }


def cubic_weights(fraction):
    return (-fraction * (fraction - 1.0) * (fraction - 2.0) / 6.0,
            (fraction + 1.0) * (fraction - 1.0) * (fraction - 2.0) / 2.0,
            -(fraction + 1.0) * fraction * (fraction - 2.0) / 2.0,
            (fraction + 1.0) * fraction * (fraction - 1.0) / 6.0)


def band_matrix(code_row, cells):
    fraction = code_row.astype(jnp.float32) / QF
    weights = cubic_weights(fraction[:, None, None])
    row_index = jnp.arange(cells)[None, :, None]
    col_index = jnp.arange(cells + 3)[None, None, :]
    total = jnp.zeros((code_row.shape[0], cells, cells + 3), jnp.float32)
    for offset in range(4):
        total = total + weights[offset] * (col_index == row_index + offset).astype(jnp.float32)
    return total


def circulant(code_row, cells):
    shift_cells = code_row // QF
    fraction = (code_row % QF).astype(jnp.float32) / QF
    weights = cubic_weights(fraction[:, None, None])
    row_index = jnp.arange(cells)[None, :, None]
    col_index = jnp.arange(cells)[None, None, :]
    total = jnp.zeros((code_row.shape[0], cells, cells), jnp.float32)
    for offset in range(4):
        target = (row_index + shift_cells[:, None, None] + offset - 1) % cells
        total = total + weights[offset] * (col_index == target).astype(jnp.float32)
    return total


def interpolate(windows, weight_rows, weight_cols, weight_depth):
    high = lax.Precision.HIGHEST
    along_depth = jnp.einsum("nabz,ncz->nabc", windows, weight_depth, precision=high)
    along_rows = jnp.einsum("nia,nabc->nibc", weight_rows, along_depth, precision=high)
    return jnp.einsum("njb,nibc->nijc", weight_cols, along_rows, precision=high)


def interpolate_adjoint(values, weight_rows, weight_cols, weight_depth):
    high = lax.Precision.HIGHEST
    along_cols = jnp.einsum("njb,nijc->nibc", weight_cols, values, precision=high)
    along_rows = jnp.einsum("nia,nibc->nabc", weight_rows, along_cols, precision=high)
    return jnp.einsum("ncz,nabc->nabz", weight_depth, along_rows, precision=high)


def gradient(field):
    parts = []
    for axis_number in range(3):
        parts.append((jnp.roll(field, -1, axis_number) - jnp.roll(field, 1, axis_number)) * 0.5)
    return jnp.stack(parts)


def reference(velocity, states, pull_plan, send_plan, codes):
    brick_a = jnp.arange(BRX)[:, None]
    brick_b = jnp.arange(BRY)[None, :]
    source_gy = pull_plan // CAP
    slot_number = pull_plan % CAP
    owner_gx = brick_a // BRX_DEV
    owner_gy = brick_b // BRY_DEV
    local_brick = send_plan[owner_gx, source_gy, owner_gy, slot_number]
    first_row = (owner_gx * BRX_DEV + local_brick // BRY_DEV) * BX
    first_col = (source_gy * BRY_DEV + local_brick % BRY_DEV) * BY
    row_index = (first_row[:, :, None] - 1 + jnp.arange(BX + 3)[None, None, :]) % NX
    col_index = (first_col[:, :, None] - 1 + jnp.arange(BY + 3)[None, None, :]) % NY
    rows_full = row_index[:, :, :, None]
    cols_full = col_index[:, :, None, :]
    count = BRX * BRY
    weight_rows = band_matrix(codes[0].reshape(count), BX)
    weight_cols = band_matrix(codes[1].reshape(count), BY)
    weight_depth = circulant(codes[2].reshape(count), CZ)

    def pull(field):
        windows = field[rows_full, cols_full].reshape(count, BX + 3, BY + 3, CZ)
        values = interpolate(windows, weight_rows, weight_cols, weight_depth)
        return values.reshape(BRX, BRY, BX, BY, CZ).transpose(0, 2, 1, 3, 4).reshape(NX, NY, CZ)

    def push(field):
        values = field.reshape(BRX, BX, BRY, BY, CZ).transpose(0, 2, 1, 3, 4).reshape(count, BX, BY, CZ)
        windows = interpolate_adjoint(values, weight_rows, weight_cols, weight_depth)
        windows = windows.reshape(BRX, BRY, BX + 3, BY + 3, CZ)
        return jnp.zeros((NX, NY, CZ), jnp.float32).at[rows_full, cols_full].add(windows)

    step_size = 1.0 / STEPS
    gradients = [gradient(states[step]) for step in range(STEPS)]
    tangent = jnp.zeros((NX, NY, CZ), jnp.float32)
    for step in range(STEPS):
        tangent = pull(tangent - step_size * jnp.sum(velocity * gradients[step], axis=0))
    adjoint = tangent
    force = jnp.zeros((3, NX, NY, CZ), jnp.float32)
    for step in reversed(range(STEPS)):
        adjoint = push(adjoint)
        force = force - step_size * adjoint[None] * gradients[step]
    return force
```

```python
import jax
import jax.numpy as jnp
from jax import lax
from jax.sharding import PartitionSpec as P

BX = 16
BY = 16
CAP = 2
QF = 8
STEPS = 2


def with_halo(cells, sides, width):
    for axis, dim in sides:
        count = lax.axis_size(axis)
        head = lax.slice_in_dim(cells, 0, width, axis=dim)
        tail = lax.slice_in_dim(cells, cells.shape[dim] - width, cells.shape[dim], axis=dim)
        cells = jnp.concatenate(
            [
                lax.ppermute(tail, axis, [(i, (i + 1) % count) for i in range(count)]),
                cells,
                lax.ppermute(head, axis, [((i + 1) % count, i) for i in range(count)]),
            ],
            axis=dim,
        )
    return cells


def cubic_weights(fraction):
    return (
        -fraction * (fraction - 1.0) * (fraction - 2.0) / 6.0,
        (fraction + 1.0) * (fraction - 1.0) * (fraction - 2.0) / 2.0,
        -(fraction + 1.0) * fraction * (fraction - 2.0) / 2.0,
        (fraction + 1.0) * fraction * (fraction - 1.0) / 6.0,
    )


def band_matrix(code_row, cells):
    fraction = code_row.astype(jnp.float32) / QF
    weights = cubic_weights(fraction[:, None, None])
    row_index = jnp.arange(cells)[None, :, None]
    col_index = jnp.arange(cells + 3)[None, None, :]
    total = jnp.zeros((code_row.shape[0], cells, cells + 3), jnp.float32)
    for offset in range(4):
        total = total + weights[offset] * (col_index == row_index + offset).astype(jnp.float32)
    return total


def circulant(code_row, cells):
    shift_cells = code_row // QF
    fraction = (code_row % QF).astype(jnp.float32) / QF
    weights = cubic_weights(fraction[:, None, None])
    row_index = jnp.arange(cells)[None, :, None]
    col_index = jnp.arange(cells)[None, None, :]
    total = jnp.zeros((code_row.shape[0], cells, cells), jnp.float32)
    for offset in range(4):
        target = (row_index + shift_cells[:, None, None] + offset - 1) % cells
        total = total + weights[offset] * (col_index == target).astype(jnp.float32)
    return total


def interpolate(windows, weight_rows, weight_cols, weight_depth):
    high = lax.Precision.HIGHEST
    along_depth = jnp.einsum("nabz,ncz->nabc", windows, weight_depth, precision=high)
    along_rows = jnp.einsum("nia,nabc->nibc", weight_rows, along_depth, precision=high)
    return jnp.einsum("njb,nibc->nijc", weight_cols, along_rows, precision=high)


def interpolate_adjoint(values, weight_rows, weight_cols, weight_depth):
    high = lax.Precision.HIGHEST
    along_cols = jnp.einsum("njb,nijc->nibc", weight_cols, values, precision=high)
    along_rows = jnp.einsum("nia,nibc->nabc", weight_rows, along_cols, precision=high)
    return jnp.einsum("ncz,nabc->nabz", weight_depth, along_rows, precision=high)


def extend(stacked):
    return with_halo(stacked, (("gx", 1), ("gy", 2)), 2)


def cut_windows(extended, brick_rows):
    pieces = []
    for row_brick in range(brick_rows):
        pieces.append(extended[row_brick * BX + 1 : row_brick * BX + BX + 4, 1 : BY + 4])
    return jnp.stack(pieces)


def place_windows(collected, brick_rows, brick_cols, rows_dev, cols_dev, depth_cells):
    accumulate = jnp.zeros((rows_dev + 4, cols_dev + 4, depth_cells), jnp.float32)
    for row_brick in range(brick_rows):
        accumulate = accumulate.at[row_brick * BX + 1 : row_brick * BX + BX + 4, 1 : BY + 4].add(
            collected[row_brick * brick_cols]
        )
    return accumulate


def fold_margins(accumulate, rows_dev, cols_dev, depth_cells):
    strips = jnp.zeros((3, rows_dev, cols_dev, depth_cells), jnp.float32)
    strips = strips.at[0, 0:2].set(accumulate[0:2, 2 : cols_dev + 2])
    strips = strips.at[0, rows_dev - 2 :].set(accumulate[rows_dev + 2 :, 2 : cols_dev + 2])
    strips = strips.at[1, :, 0:2].set(accumulate[2 : rows_dev + 2, 0:2])
    strips = strips.at[1, :, cols_dev - 2 :].set(accumulate[2 : rows_dev + 2, cols_dev + 2 :])
    strips = strips.at[2, 0:2, 0:2].set(accumulate[0:2, 0:2])
    strips = strips.at[2, 0:2, cols_dev - 2 :].set(accumulate[0:2, cols_dev + 2 :])
    strips = strips.at[2, rows_dev - 2 :, 0:2].set(accumulate[rows_dev + 2 :, 0:2])
    strips = strips.at[2, rows_dev - 2 :, cols_dev - 2 :].set(
        accumulate[rows_dev + 2 :, cols_dev + 2 :]
    )
    arrived = with_halo(strips, (("gx", 1), ("gy", 2)), 2)
    result = accumulate[2 : rows_dev + 2, 2 : cols_dev + 2]
    result = result.at[0:2].add(arrived[0, 0:2, 2 : cols_dev + 2])
    result = result.at[rows_dev - 2 :].add(arrived[0, rows_dev + 2 :, 2 : cols_dev + 2])
    result = result.at[:, 0:2].add(arrived[1, 2 : rows_dev + 2, 0:2])
    result = result.at[:, cols_dev - 2 :].add(arrived[1, 2 : rows_dev + 2, cols_dev + 2 :])
    result = result.at[0:2, 0:2].add(arrived[2, 0:2, 0:2])
    result = result.at[0:2, cols_dev - 2 :].add(arrived[2, 0:2, cols_dev + 2 :])
    result = result.at[rows_dev - 2 :, 0:2].add(arrived[2, rows_dev + 2 :, 0:2])
    result = result.at[rows_dev - 2 :, cols_dev - 2 :].add(
        arrived[2, rows_dev + 2 :, cols_dev + 2 :]
    )
    return result


def body(velocity, states, pull_plan, send_plan, codes):
    rows_dev = velocity.shape[1]
    cols_dev = velocity.shape[2]
    depth_cells = velocity.shape[3]
    brick_rows = rows_dev // BX
    brick_cols = cols_dev // BY
    bricks = brick_rows * brick_cols
    peer_count = lax.axis_size("gy")
    slot_count = peer_count * CAP
    step_size = 1.0 / STEPS
    high = lax.Precision.HIGHEST
    pull_flat = pull_plan.reshape(bricks)
    owners = send_plan.reshape(slot_count)
    send_flat = jnp.maximum(owners, 0)
    code_flat = codes.reshape(3, bricks)
    selector = (owners[None, :] == jnp.arange(bricks)[:, None]).astype(jnp.float32)
    request = jnp.zeros((slot_count, 3), jnp.int32).at[pull_flat].set(code_flat.T)
    requested = lax.all_to_all(
        request.reshape(peer_count, CAP, 3), "gy", split_axis=0, concat_axis=0, tiled=True
    ).reshape(slot_count, 3)
    weight_rows = band_matrix(requested[:, 0], BX)
    weight_cols = band_matrix(requested[:, 1], BY)
    weight_depth = circulant(requested[:, 2], depth_cells)
    extended_states = extend(states)
    centre = extended_states[:, 2 : rows_dev + 2, 2 : cols_dev + 2]
    grad_rows = (
        extended_states[:, 3 : rows_dev + 3, 2 : cols_dev + 2]
        - extended_states[:, 1 : rows_dev + 1, 2 : cols_dev + 2]
    ) * 0.5
    grad_cols = (
        extended_states[:, 2 : rows_dev + 2, 3 : cols_dev + 3]
        - extended_states[:, 2 : rows_dev + 2, 1 : cols_dev + 1]
    ) * 0.5
    grad_depth = (jnp.roll(centre, -1, 3) - jnp.roll(centre, 1, 3)) * 0.5
    gradients = jnp.stack([grad_rows, grad_cols, grad_depth], axis=1)
    tangent = jnp.zeros((rows_dev, cols_dev, depth_cells), jnp.float32)
    for step in range(STEPS):
        extended = extend(
            (tangent - step_size * jnp.sum(velocity * gradients[step], axis=0))[None]
        )[0]
        windows = cut_windows(extended, brick_rows)
        supplied = interpolate(
            jnp.take(windows, send_flat, axis=0), weight_rows, weight_cols, weight_depth
        )
        if step == STEPS - 1:
            break
        pull_inbox = lax.all_to_all(
            supplied.reshape(peer_count, CAP, BX, BY, depth_cells),
            "gy",
            split_axis=0,
            concat_axis=0,
            tiled=True,
        ).reshape(slot_count, BX, BY, depth_cells)
        tangent = (
            jnp.take(pull_inbox, pull_flat, axis=0)
            .reshape(brick_rows, brick_cols, BX, BY, depth_cells)
            .transpose(0, 2, 1, 3, 4)
            .reshape(rows_dev, cols_dev, depth_cells)
        )
    inbox = supplied
    force = jnp.zeros((3, rows_dev, cols_dev, depth_cells), jnp.float32)
    for step in reversed(range(STEPS)):
        if step < STEPS - 1:
            outbox = (
                jnp.zeros((slot_count, BX, BY, depth_cells), jnp.float32)
                .at[pull_flat]
                .set(
                    adjoint.reshape(brick_rows, BX, brick_cols, BY, depth_cells)
                    .transpose(0, 2, 1, 3, 4)
                    .reshape(bricks, BX, BY, depth_cells)
                )
                .reshape(peer_count, CAP, BX, BY, depth_cells)
            )
            inbox = lax.all_to_all(outbox, "gy", split_axis=0, concat_axis=0, tiled=True).reshape(
                slot_count, BX, BY, depth_cells
            )
        collected = jnp.einsum(
            "ks,sabz->kabz",
            selector,
            interpolate_adjoint(inbox, weight_rows, weight_cols, weight_depth),
            precision=high,
        )
        accumulate = place_windows(
            collected, brick_rows, brick_cols, rows_dev, cols_dev, depth_cells
        )
        adjoint = fold_margins(accumulate, rows_dev, cols_dev, depth_cells)
        force = force - step_size * adjoint[None] * gradients[step]
    return force


def solution(mesh):
    return jax.shard_map(
        body,
        mesh=mesh,
        in_specs=(
            P(None, "gx", "gy", None),
            P(None, "gx", "gy", None),
            P("gx", "gy"),
            P("gx", "gy", None, None),
            P(None, "gx", "gy"),
        ),
        out_specs=P(None, "gx", "gy", None),
        check_vma=False,
    )
```

```python
import functools

import jax
import jax.numpy as jnp
from jax import lax
from jax.experimental import pallas as pl
from jax.experimental.pallas import tpu as pltpu
from jax.sharding import PartitionSpec as P

BX = 16
BY = 16
CAP = 2
QF = 8
STEPS = 2
STEP_SIZE = 1.0 / STEPS
WIN = BX + 3
LANES = 24
VMEM_LIMIT = 40 * 1024 * 1024
F32 = jnp.float32


def shape(*dims):
    return jax.ShapeDtypeStruct(dims, F32)


def exchange(name, collective_id, operands, out_shapes, plan):
    n_gx, n_gy = lax.axis_size("gx"), lax.axis_size("gy")
    count = len(operands)

    def kernel(*refs):
        ins = refs[:count]
        outs = refs[count : count + len(out_shapes)]
        send_sem, recv_sem, local_sem = refs[count + len(out_shapes) :]
        gx, gy = lax.axis_index("gx"), lax.axis_index("gy")

        def device(step_x, step_y):
            return (lax.rem(gx + step_x + n_gx, n_gx), lax.rem(gy + step_y + n_gy, n_gy))

        remote, local, peers = plan(ins, outs, gy, n_gy)
        barrier = pltpu.get_barrier_semaphore()
        for peer in peers:
            pl.semaphore_signal(
                barrier, inc=1, device_id=device(*peer), device_id_type=pl.DeviceIdType.MESH
            )
        own = [
            pltpu.make_async_copy(src, dst, local_sem.at[i]) for i, (src, dst) in enumerate(local)
        ]
        for copy in own:
            copy.start()
        pl.semaphore_wait(barrier, len(peers))
        copies = []
        for i, (src, dst, step_x, step_y) in enumerate(remote):
            copy = pltpu.make_async_remote_copy(
                src_ref=src,
                dst_ref=dst,
                send_sem=send_sem.at[i],
                recv_sem=recv_sem.at[i],
                device_id=device(step_x, step_y),
                device_id_type=pl.DeviceIdType.MESH,
            )
            copy.start()
            copies.append(copy)
        for copy in own:
            copy.wait()
        for copy in copies:
            copy.wait()

    slots = 3 * n_gy + 8
    return pl.pallas_call(
        kernel,
        name=name,
        out_shape=out_shapes,
        in_specs=[pl.BlockSpec(memory_space=pl.ANY)] * count,
        out_specs=[pl.BlockSpec(memory_space=pl.ANY)] * len(out_shapes),
        scratch_shapes=[
            pltpu.SemaphoreType.DMA((slots,)),
            pltpu.SemaphoreType.DMA((slots,)),
            pltpu.SemaphoreType.DMA((2,)),
        ],
        compiler_params=pltpu.CompilerParams(
            collective_id=collective_id, has_side_effects=True, vmem_limit_bytes=VMEM_LIMIT
        ),
    )(*operands)


NEIGHBOURS = [(i, j) for i in (-1, 0, 1) for j in (-1, 0, 1) if (i, j) != (0, 0)]


def states_plan(ins, outs, gy, n_gy):
    rows, cols, request = ins
    rows_in, cols_in, requested = outs
    remote = [
        (rows.at[0], rows_in.at[0], 1, 0),
        (rows.at[1], rows_in.at[1], -1, 0),
        (cols.at[0], cols_in.at[0], 0, 1),
        (cols.at[1], cols_in.at[1], 0, -1),
    ]
    for step in range(1, n_gy):
        peer = lax.rem(gy + step, n_gy)
        remote.append((request.at[peer], requested.at[gy], 0, step))
    local = [(request.at[gy], requested.at[gy])]
    return remote, local, [(1, 0), (-1, 0)] + [(0, step) for step in range(1, n_gy)]


def halo_plan(ins, outs, gy, n_gy):
    field, cols = ins
    rows_in, cols_in = outs
    rows = field.shape[0]
    main, low, high = pl.ds(8, rows), pl.ds(0, 8), pl.ds(rows + 8, 8)
    first, last = pl.ds(0, 8), pl.ds(rows - 8, 8)
    one, two = pl.ds(0, 1), pl.ds(1, 2)
    remote = [
        (cols.at[one], cols_in.at[one, main], 0, 1),
        (cols.at[two], cols_in.at[two, main], 0, -1),
        (field.at[pl.ds(rows - 1, 1)], rows_in.at[one], 1, 0),
        (field.at[pl.ds(0, 2)], rows_in.at[two], -1, 0),
        (cols.at[one, last], cols_in.at[one, low], 1, 1),
        (cols.at[one, first], cols_in.at[one, high], -1, 1),
        (cols.at[two, last], cols_in.at[two, low], 1, -1),
        (cols.at[two, first], cols_in.at[two, high], -1, -1),
    ]
    return remote, [], NEIGHBOURS


def fold_plan(ins, outs, gy, n_gy):
    rows_out, cols = ins
    rows_in, cols_in = outs
    rows = cols.shape[1] - 16
    main, low, high = pl.ds(8, rows), pl.ds(0, 8), pl.ds(rows + 8, 8)
    one, two = pl.ds(0, 1), pl.ds(1, 2)
    remote = [
        (cols.at[one, main], cols_in.at[one, main], 0, -1),
        (cols.at[two, main], cols_in.at[two, main], 0, 1),
        (rows_out.at[one], rows_in.at[one], -1, 0),
        (rows_out.at[two], rows_in.at[two], 1, 0),
        (cols.at[one, low], cols_in.at[one, high], -1, -1),
        (cols.at[one, high], cols_in.at[one, low], 1, -1),
        (cols.at[two, low], cols_in.at[two, high], -1, 1),
        (cols.at[two, high], cols_in.at[two, low], 1, 1),
    ]
    return remote, [], NEIGHBOURS


def bricks_plan(ins, outs, gy, n_gy):
    (outbox,), (inbox,) = ins, outs
    mine = pl.ds(gy * CAP, CAP)
    remote = []
    for step in range(1, n_gy):
        peer = lax.rem(gy + step, n_gy)
        remote.append((outbox.at[pl.ds(peer * CAP, CAP)], inbox.at[mine], 0, step))
    return remote, [(outbox.at[mine], inbox.at[mine])], [(0, step) for step in range(1, n_gy)]


def cubic_weights(f):
    return (
        -f * (f - 1.0) * (f - 2.0) * (1.0 / 6.0),
        (f + 1.0) * (f - 1.0) * (f - 2.0) * 0.5,
        -(f + 1.0) * f * (f - 2.0) * 0.5,
        (f + 1.0) * f * (f - 1.0) * (1.0 / 6.0),
    )


def slot_weights(codes, slot):
    u, v, q = codes[3 * slot], codes[3 * slot + 1], codes[3 * slot + 2]
    depth_shift = lax.shift_right_logical(q, 3)
    fractions = [u, v, jnp.bitwise_and(q, QF - 1)]
    return depth_shift, [cubic_weights(f.astype(F32) * (1.0 / QF)) for f in fractions]


def weighted(weights, terms):
    total = weights[0] * terms[0]
    for weight, term in zip(weights[1:], terms[1:]):
        total = total + weight * term
    return total


def pull_brick(window, shift, weights):
    depth = window.shape[2]
    rows = weighted(weights[0], [window[r : r + BX] for r in range(4)])
    cols = weighted(
        weights[1],
        [(rows if t == 0 else pltpu.roll(rows, LANES - t, 1))[:, :BY] for t in range(4)],
    )
    base = pltpu.roll(cols, lax.rem(depth + 1 - shift, depth), 2)
    return weighted(
        weights[2], [base if m == 0 else pltpu.roll(base, depth - m, 2) for m in range(4)]
    )


def push_brick(values, shift, weights):
    depth = values.shape[2]
    base = pltpu.roll(values, lax.rem(depth - 1 + shift, depth), 2)
    along = weighted(weights[2], [base if m == 0 else pltpu.roll(base, m, 2) for m in range(4)])
    wide = jnp.concatenate([along, jnp.zeros((BX, LANES - BY, depth), F32)], axis=1)
    cols = weighted(weights[1], [wide if t == 0 else pltpu.roll(wide, t, 1) for t in range(4)])
    parts = []
    for r in range(4):
        pieces = [cols * weights[0][r]]
        if r > 0:
            pieces.insert(0, jnp.zeros((r, LANES, depth), F32))
        if r < 3:
            pieces.append(jnp.zeros((3 - r, LANES, depth), F32))
        parts.append(jnp.concatenate(pieces, axis=0))
    return parts[0] + parts[1] + parts[2] + parts[3]


def assemble(extended, field, rows_in, cols_in):
    rows = field.shape[0]
    extended[1 : rows + 1, 1 : BY + 1, :] = field[...]
    extended[0:1, 1 : BY + 1, :] = rows_in[0:1]
    extended[rows + 1 : rows + 3, 1 : BY + 1, :] = rows_in[1:3]
    for col, side in ((0, 0), (BY + 1, 1), (BY + 2, 2)):
        extended[:, col, :] = cols_in[side, 7 : rows + 10, :]


def emit_margins(total, acc, rows_out, cols_out):
    rows = total.shape[0]
    total[...] = acc[1 : rows + 1, 1 : BY + 1, :]
    rows_out[0:1] = acc[0:1, 1 : BY + 1, :]
    rows_out[1:3] = acc[rows + 1 : rows + 3, 1 : BY + 1, :]
    cols_out[...] = jnp.zeros_like(cols_out)
    for col, side in ((0, 0), (BY + 1, 1), (BY + 2, 2)):
        cols_out[side, 7 : rows + 10, :] = acc[:, col, :]


def pull_kernel(owners, codes, field, rows_in, cols_in, out, extended):
    slot = pl.program_id(0)

    @pl.when(slot == 0)
    def _():
        assemble(extended, field, rows_in, cols_in)

    owner = owners[slot]

    @pl.when(owner >= 0)
    def _():
        shift, weights = slot_weights(codes, slot)
        out[0] = pull_brick(extended[pl.ds(owner * BX, WIN)], shift, weights)


def pull_push_kernel(
    owners, codes, field, rows_in, cols_in, total, rows_out, cols_out, extended, acc
):
    slot = pl.program_id(0)

    @pl.when(slot == 0)
    def _():
        assemble(extended, field, rows_in, cols_in)
        acc[...] = jnp.zeros_like(acc)

    owner = owners[slot]

    @pl.when(owner >= 0)
    def _():
        shift, weights = slot_weights(codes, slot)
        window = pl.ds(owner * BX, WIN)
        brick = pull_brick(extended[window], shift, weights)
        acc[window] = acc[window] + push_brick(brick, shift, weights)

    @pl.when(slot == pl.num_programs(0) - 1)
    def _():
        emit_margins(total, acc, rows_out, cols_out)


def push_kernel(owners, codes, inbox, total, rows_out, cols_out, acc):
    slot = pl.program_id(0)

    @pl.when(slot == 0)
    def _():
        acc[...] = jnp.zeros_like(acc)

    owner = owners[slot]

    @pl.when(owner >= 0)
    def _():
        shift, weights = slot_weights(codes, slot)
        window = pl.ds(owner * BX, WIN)
        acc[window] = acc[window] + push_brick(inbox[0], shift, weights)

    @pl.when(slot == pl.num_programs(0) - 1)
    def _():
        emit_margins(total, acc, rows_out, cols_out)


def gradient(states, rows_in, cols_in, step, block, blocks):
    rows, depth = states.shape[1], states.shape[3]
    first = block * BX
    cells = states[step, pl.ds(first, BX)]
    before = states[step, pl.ds(jnp.maximum(first - 1, 0), 1)]
    after = states[step, pl.ds(jnp.minimum(first + BX, rows - 1), 1)]
    before = jnp.where(block == 0, rows_in[0, pl.ds(step, 1)], before)
    after = jnp.where(block == blocks - 1, rows_in[1, pl.ds(step, 1)], after)
    left = cols_in[0, step, pl.ds(first, BX)][:, None, :]
    right = cols_in[1, step, pl.ds(first, BX)][:, None, :]
    col = lax.broadcasted_iota(jnp.int32, cells.shape, 1)
    below = jnp.concatenate([before, cells[:-1]], axis=0)
    above = jnp.concatenate([cells[1:], after], axis=0)
    lower = jnp.where(col == 0, left, pltpu.roll(cells, 1, 1))
    upper = jnp.where(col == BY - 1, right, pltpu.roll(cells, BY - 1, 1))
    return (
        (above - below) * 0.5,
        (upper - lower) * 0.5,
        (pltpu.roll(cells, depth - 1, 2) - pltpu.roll(cells, 1, 2)) * 0.5,
    )


def emit_field(values, field, cols):
    field[...] = values
    for side, col in ((0, BY - 1), (1, 0), (2, 1)):
        cols[side] = values[:, col, :]


def source_kernel(states, rows_in, cols_in, velocity, field, cols, later):
    block, blocks = pl.program_id(0), pl.num_programs(0)
    terms = []
    for step in range(STEPS):
        parts = gradient(states, rows_in, cols_in, step, block, blocks)
        terms.append(
            (velocity[0] * parts[0] + velocity[1] * parts[1] + velocity[2] * parts[2]) * -STEP_SIZE
        )
    emit_field(terms[0], field, cols)
    later[...] = terms[1]


def tangent_kernel(pulls, inbox, later, field, cols):
    emit_field(inbox[0] + later[...], field, cols)


def fold(total, rows_in, cols_in):
    block, blocks = pl.program_id(0), pl.num_programs(0)
    depth = total.shape[2]
    is_first, is_last = block == 0, block == blocks - 1
    rows = cols_in.shape[1] - 16
    zeros = jnp.zeros((8, depth), F32)
    values = total[...]
    col = lax.broadcasted_iota(jnp.int32, values.shape, 1)
    row = lax.broadcasted_iota(jnp.int32, values.shape, 0)
    values = values + jnp.where(jnp.logical_and(is_last, row == BX - 1), rows_in[0:1], 0.0)
    for i in range(2):
        values = values + jnp.where(
            jnp.logical_and(is_first, row == i), rows_in[1 + i : 2 + i], 0.0
        )
    for side, place in ((0, BY - 1), (1, 0), (2, 1)):
        strip = cols_in[side, pl.ds(8 + block * BX, BX)]
        low = jnp.concatenate([cols_in[side, 0:8], zeros], axis=0)
        high = jnp.concatenate([zeros, cols_in[side, rows + 8 : rows + 16]], axis=0)
        strip = strip + jnp.where(is_first, low, 0.0) + jnp.where(is_last, high, 0.0)
        values = values + jnp.where(col == place, strip[:, None, :], 0.0)
    return values


def outbox_kernel(pulls, total, rows_in, cols_in, adjoint, outbox):
    values = fold(total, rows_in, cols_in)
    adjoint[...] = values
    outbox[0] = values


def force_kernel(
    states, rows_in, cols_in, later_adjoint, total, fold_rows, fold_cols, force
):
    block, blocks = pl.program_id(0), pl.num_programs(0)
    adjoints = [fold(total, fold_rows, fold_cols), later_adjoint[...]]
    scaled = [adjoint * -STEP_SIZE for adjoint in adjoints]
    early = gradient(states, rows_in, cols_in, 0, block, blocks)
    late = gradient(states, rows_in, cols_in, 1, block, blocks)
    for c in range(3):
        force[c] = scaled[1] * late[c] + scaled[0] * early[c]


def whole(dims):
    return pl.BlockSpec(dims, lambda *_: (0,) * len(dims))


def local_call(kernel, name, steps, scalars, in_specs, out_specs, out_shapes, scratch, operands):
    return pl.pallas_call(
        kernel,
        name=name,
        grid_spec=pltpu.PrefetchScalarGridSpec(
            num_scalar_prefetch=len(scalars),
            grid=(steps,),
            in_specs=in_specs,
            out_specs=out_specs,
            scratch_shapes=scratch,
        ),
        out_shape=out_shapes,
        compiler_params=pltpu.CompilerParams(vmem_limit_bytes=VMEM_LIMIT),
    )(*scalars, *operands)


def body(velocity, states, pull_plan, send_plan, codes):
    _, rows, cols, depth = velocity.shape
    assert cols == BY and rows % BX == 0
    bricks = rows // BX
    peers = lax.axis_size("gy")
    slots = peers * CAP
    pulls = pull_plan.reshape(bricks)
    owners = send_plan.reshape(slots)
    code_flat = codes.reshape(3, bricks)

    match = pulls[None, :] == jnp.arange(slots, dtype=jnp.int32)[:, None]
    request = jnp.sum(jnp.where(match[:, None, :], code_flat[None], 0), axis=2)
    request = jnp.pad(request.reshape(peers, CAP, 3), ((0, 0), (0, 8 - CAP), (0, 125)))
    edge_rows = jnp.stack([states[:, rows - 1], states[:, 0]])
    edge_cols = jnp.stack([states[:, :, cols - 1], states[:, :, 0]])
    state_rows, state_cols, requested = exchange(
        "exchange_states",
        0,
        (edge_rows, edge_cols, request),
        [
            shape(2, STEPS, cols, depth),
            shape(2, STEPS, rows, depth),
            jax.ShapeDtypeStruct((peers, 8, 128), jnp.int32),
        ],
        states_plan,
    )
    slot_codes = requested[:, :CAP, :3].reshape(slots * 3)

    block = pl.BlockSpec((BX, BY, depth), lambda k, *_: (k, 0, 0))
    vector_block = pl.BlockSpec((3, BX, BY, depth), lambda k, *_: (0, k, 0, 0))
    edge_block = pl.BlockSpec((3, BX, depth), lambda k, *_: (0, k, 0))
    slot_block = pl.BlockSpec((1, BX, BY, depth), lambda s, *_: (s, 0, 0, 0))
    named_block = pl.BlockSpec((1, BX, BY, depth), lambda k, plan: (plan[k], 0, 0, 0))
    state_specs = [whole(states.shape), whole(state_rows.shape), whole(state_cols.shape)]
    field_shape = shape(rows, cols, depth)
    edge_shape = shape(3, rows, depth)
    margin_shapes = [shape(3, cols, depth), shape(3, rows + 16, depth)]
    margin_specs = [whole(s.shape) for s in margin_shapes]
    field_spec = whole(field_shape.shape)
    slot_shape = shape(slots, BX, BY, depth)
    extended = pltpu.VMEM((rows + 3, LANES, depth), F32)

    field, edges, later = local_call(
        source_kernel, "source", bricks, (), state_specs + [vector_block],
        [block, edge_block, block], [field_shape, edge_shape, field_shape], [],
        (states, state_rows, state_cols, velocity),
    )
    halo = exchange("exchange_source", 1, (field, edges), margin_shapes, halo_plan)
    supplied = local_call(
        pull_kernel, "pull", slots, (owners, slot_codes), [field_spec] + margin_specs,
        slot_block, slot_shape, [extended], (field, *halo),
    )
    (inbox,) = exchange("exchange_pulled", 2, (supplied,), [slot_shape], bricks_plan)
    field, edges = local_call(
        tangent_kernel, "tangent", bricks, (pulls,), [named_block, block],
        [block, edge_block], [field_shape, edge_shape], [], (inbox, later),
    )
    halo = exchange("exchange_tangent", 3, (field, edges), margin_shapes, halo_plan)
    total, *margins = local_call(
        pull_push_kernel, "pull_push", slots, (owners, slot_codes), [field_spec] + margin_specs,
        [field_spec] + margin_specs, [field_shape] + margin_shapes, [extended, extended],
        (field, *halo),
    )
    margins = exchange("fold_late", 4, margins, margin_shapes, fold_plan)
    late_adjoint, outbox = local_call(
        outbox_kernel, "outbox", bricks, (pulls,), [block] + margin_specs,
        [block, named_block], [field_shape, slot_shape], [], (total, *margins),
    )
    (inbox,) = exchange("exchange_adjoint", 5, (outbox,), [slot_shape], bricks_plan)
    total, *margins = local_call(
        push_kernel, "push", slots, (owners, slot_codes), [slot_block],
        [field_spec] + margin_specs, [field_shape] + margin_shapes, [extended], (inbox,),
    )
    margins = exchange("fold_early", 6, margins, margin_shapes, fold_plan)
    return local_call(
        force_kernel, "force", bricks, (), state_specs + [block, block] + margin_specs,
        vector_block, shape(3, rows, cols, depth), [],
        (states, state_rows, state_cols, late_adjoint, total, *margins),
    )


def solution(mesh):
    return jax.shard_map(
        body,
        mesh=mesh,
        in_specs=(
            P(None, "gx", "gy", None),
            P(None, "gx", "gy", None),
            P("gx", "gy"),
            P("gx", "gy", None, None),
            P(None, "gx", "gy"),
        ),
        out_specs=P(None, "gx", "gy", None),
        check_vma=False,
    )
```

```python
import functools

import jax
import jax.numpy as jnp
from jax import lax
from jax.experimental import pallas as pl
from jax.experimental.pallas import tpu as pltpu
from jax.sharding import PartitionSpec as P

BX = 16
BY = 16
CAP = 2
QF = 8
STEPS = 2
STEP_SIZE = 1.0 / STEPS
WIN = BX + 3
LANES = 24
VMEM_LIMIT = 40 * 1024 * 1024
F32 = jnp.float32


def shape(*dims):
    return jax.ShapeDtypeStruct(dims, F32)


def exchange(name, collective_id, operands, out_shapes, plan):
    n_gx, n_gy = lax.axis_size("gx"), lax.axis_size("gy")
    count = len(operands)

    def kernel(*refs):
        ins = refs[:count]
        outs = refs[count : count + len(out_shapes)]
        send_sem, recv_sem, local_sem = refs[count + len(out_shapes) :]
        gx, gy = lax.axis_index("gx"), lax.axis_index("gy")

        def device(step_x, step_y):
            return (lax.rem(gx + step_x + n_gx, n_gx), lax.rem(gy + step_y + n_gy, n_gy))

        remote, local, peers = plan(ins, outs, gy, n_gy)
        barrier = pltpu.get_barrier_semaphore()
        for peer in peers:
            pl.semaphore_signal(
                barrier, inc=1, device_id=device(*peer), device_id_type=pl.DeviceIdType.MESH
            )
        own = [
            pltpu.make_async_copy(src, dst, local_sem.at[i]) for i, (src, dst) in enumerate(local)
        ]
        for copy in own:
            copy.start()
        pl.semaphore_wait(barrier, len(peers))
        copies = []
        for i, (src, dst, step_x, step_y) in enumerate(remote):
            copy = pltpu.make_async_remote_copy(
                src_ref=src,
                dst_ref=dst,
                send_sem=send_sem.at[i],
                recv_sem=recv_sem.at[i],
                device_id=device(step_x, step_y),
                device_id_type=pl.DeviceIdType.MESH,
            )
            copy.start()
            copies.append(copy)
        for copy in own:
            copy.wait()
        for copy in copies:
            copy.wait()

    slots = 3 * n_gy + 8
    return pl.pallas_call(
        kernel,
        name=name,
        out_shape=out_shapes,
        in_specs=[pl.BlockSpec(memory_space=pl.ANY)] * count,
        out_specs=[pl.BlockSpec(memory_space=pl.ANY)] * len(out_shapes),
        scratch_shapes=[
            pltpu.SemaphoreType.DMA((slots,)),
            pltpu.SemaphoreType.DMA((slots,)),
            pltpu.SemaphoreType.DMA((2,)),
        ],
        compiler_params=pltpu.CompilerParams(
            collective_id=collective_id, has_side_effects=True, vmem_limit_bytes=VMEM_LIMIT
        ),
    )(*operands)


NEIGHBOURS = [(i, j) for i in (-1, 0, 1) for j in (-1, 0, 1) if (i, j) != (0, 0)]


def halo_plan(ins, outs, gy, n_gy):
    field, cols = ins
    rows_in, cols_in = outs
    rows = field.shape[0]
    main, low, high = pl.ds(8, rows), pl.ds(0, 8), pl.ds(rows + 8, 8)
    first, last = pl.ds(0, 8), pl.ds(rows - 8, 8)
    one, two = pl.ds(0, 1), pl.ds(1, 2)
    remote = [
        (cols.at[one], cols_in.at[one, main], 0, 1),
        (cols.at[two], cols_in.at[two, main], 0, -1),
        (field.at[pl.ds(rows - 1, 1)], rows_in.at[one], 1, 0),
        (field.at[pl.ds(0, 2)], rows_in.at[two], -1, 0),
        (cols.at[one, last], cols_in.at[one, low], 1, 1),
        (cols.at[one, first], cols_in.at[one, high], -1, 1),
        (cols.at[two, last], cols_in.at[two, low], 1, -1),
        (cols.at[two, first], cols_in.at[two, high], -1, -1),
    ]
    return remote, [], NEIGHBOURS


def fold_plan(ins, outs, gy, n_gy):
    rows_out, cols = ins
    rows_in, cols_in = outs
    rows = cols.shape[1] - 16
    main, low, high = pl.ds(8, rows), pl.ds(0, 8), pl.ds(rows + 8, 8)
    one, two = pl.ds(0, 1), pl.ds(1, 2)
    remote = [
        (cols.at[one, main], cols_in.at[one, main], 0, -1),
        (cols.at[two, main], cols_in.at[two, main], 0, 1),
        (rows_out.at[one], rows_in.at[one], -1, 0),
        (rows_out.at[two], rows_in.at[two], 1, 0),
        (cols.at[one, low], cols_in.at[one, high], -1, -1),
        (cols.at[one, high], cols_in.at[one, low], 1, -1),
        (cols.at[two, low], cols_in.at[two, high], -1, 1),
        (cols.at[two, high], cols_in.at[two, low], 1, 1),
    ]
    return remote, [], NEIGHBOURS


def bricks_plan(ins, outs, gy, n_gy):
    (outbox,), (inbox,) = ins, outs
    mine = pl.ds(gy * CAP, CAP)
    remote = []
    for step in range(1, n_gy):
        peer = lax.rem(gy + step, n_gy)
        remote.append((outbox.at[pl.ds(peer * CAP, CAP)], inbox.at[mine], 0, step))
    return remote, [(outbox.at[mine], inbox.at[mine])], [(0, step) for step in range(1, n_gy)]


def cubic_weights(f):
    return (
        -f * (f - 1.0) * (f - 2.0) * (1.0 / 6.0),
        (f + 1.0) * (f - 1.0) * (f - 2.0) * 0.5,
        -(f + 1.0) * f * (f - 2.0) * 0.5,
        (f + 1.0) * f * (f - 1.0) * (1.0 / 6.0),
    )


def code_weights(u, v, q):
    depth_shift = lax.shift_right_logical(q, 3)
    fractions = [u, v, jnp.bitwise_and(q, QF - 1)]
    return depth_shift, [cubic_weights(f.astype(F32) * (1.0 / QF)) for f in fractions]


def slot_weights(codes, slot):
    return code_weights(codes[3 * slot], codes[3 * slot + 1], codes[3 * slot + 2])


def weighted(weights, terms):
    total = weights[0] * terms[0]
    for weight, term in zip(weights[1:], terms[1:]):
        total = total + weight * term
    return total


def pull_brick(window, shift, weights):
    depth = window.shape[2]
    rows = weighted(weights[0], [window[r : r + BX] for r in range(4)])
    cols = weighted(
        weights[1],
        [(rows if t == 0 else pltpu.roll(rows, LANES - t, 1))[:, :BY] for t in range(4)],
    )
    base = pltpu.roll(cols, lax.rem(depth + 1 - shift, depth), 2)
    return weighted(
        weights[2], [base if m == 0 else pltpu.roll(base, depth - m, 2) for m in range(4)]
    )


def push_brick(values, shift, weights):
    depth = values.shape[2]
    base = pltpu.roll(values, lax.rem(depth - 1 + shift, depth), 2)
    along = weighted(weights[2], [base if m == 0 else pltpu.roll(base, m, 2) for m in range(4)])
    wide = jnp.concatenate([along, jnp.zeros((BX, LANES - BY, depth), F32)], axis=1)
    cols = weighted(weights[1], [wide if t == 0 else pltpu.roll(wide, t, 1) for t in range(4)])
    parts = []
    for r in range(4):
        pieces = [cols * weights[0][r]]
        if r > 0:
            pieces.insert(0, jnp.zeros((r, LANES, depth), F32))
        if r < 3:
            pieces.append(jnp.zeros((3 - r, LANES, depth), F32))
        parts.append(jnp.concatenate(pieces, axis=0))
    return parts[0] + parts[1] + parts[2] + parts[3]


def assemble(extended, field, rows_in, cols_in):
    rows = field.shape[0]
    extended[1 : rows + 1, 1 : BY + 1, :] = field[...]
    extended[0:1, 1 : BY + 1, :] = rows_in[0:1]
    extended[rows + 1 : rows + 3, 1 : BY + 1, :] = rows_in[1:3]
    for col, side in ((0, 0), (BY + 1, 1), (BY + 2, 2)):
        extended[:, col, :] = cols_in[side, 7 : rows + 10, :]


def emit_margins(total, acc, rows_out, cols_out):
    rows = total.shape[0]
    total[...] = acc[1 : rows + 1, 1 : BY + 1, :]
    rows_out[0:1] = acc[0:1, 1 : BY + 1, :]
    rows_out[1:3] = acc[rows + 1 : rows + 3, 1 : BY + 1, :]
    cols_out[...] = jnp.zeros_like(cols_out)
    for col, side in ((0, 0), (BY + 1, 1), (BY + 2, 2)):
        cols_out[side, 7 : rows + 10, :] = acc[:, col, :]


def pull_push_kernel(
    owners, codes, field, rows_in, cols_in, total, rows_out, cols_out, extended, acc
):
    slot = pl.program_id(0)

    @pl.when(slot == 0)
    def _():
        assemble(extended, field, rows_in, cols_in)
        acc[...] = jnp.zeros_like(acc)

    owner = owners[slot]

    @pl.when(owner >= 0)
    def _():
        shift, weights = slot_weights(codes, slot)
        window = pl.ds(owner * BX, WIN)
        brick = pull_brick(extended[window], shift, weights)
        acc[window] = acc[window] + push_brick(brick, shift, weights)

    @pl.when(slot == pl.num_programs(0) - 1)
    def _():
        emit_margins(total, acc, rows_out, cols_out)


def push_kernel(owners, codes, inbox, total, rows_out, cols_out, acc):
    slot = pl.program_id(0)

    @pl.when(slot == 0)
    def _():
        acc[...] = jnp.zeros_like(acc)

    owner = owners[slot]

    @pl.when(owner >= 0)
    def _():
        shift, weights = slot_weights(codes, slot)
        window = pl.ds(owner * BX, WIN)
        acc[window] = acc[window] + push_brick(inbox[0], shift, weights)

    @pl.when(slot == pl.num_programs(0) - 1)
    def _():
        emit_margins(total, acc, rows_out, cols_out)


def gradient(states, rows_in, cols_in, step, block, blocks):
    rows, depth = states.shape[1], states.shape[3]
    first = block * BX
    cells = states[step, pl.ds(first, BX)]
    before = states[step, pl.ds(jnp.maximum(first - 1, 0), 1)]
    after = states[step, pl.ds(jnp.minimum(first + BX, rows - 1), 1)]
    before = jnp.where(block == 0, rows_in[0, pl.ds(step, 1)], before)
    after = jnp.where(block == blocks - 1, rows_in[1, pl.ds(step, 1)], after)
    left = cols_in[0, step, pl.ds(first, BX)][:, None, :]
    right = cols_in[1, step, pl.ds(first, BX)][:, None, :]
    col = lax.broadcasted_iota(jnp.int32, cells.shape, 1)
    below = jnp.concatenate([before, cells[:-1]], axis=0)
    above = jnp.concatenate([cells[1:], after], axis=0)
    lower = jnp.where(col == 0, left, pltpu.roll(cells, 1, 1))
    upper = jnp.where(col == BY - 1, right, pltpu.roll(cells, BY - 1, 1))
    return (
        (above - below) * 0.5,
        (upper - lower) * 0.5,
        (pltpu.roll(cells, depth - 1, 2) - pltpu.roll(cells, 1, 2)) * 0.5,
    )


def emit_field(values, field, cols):
    field[...] = values
    for side, col in ((0, BY - 1), (1, 0), (2, 1)):
        cols[side] = values[:, col, :]


def supply_kernel(
    n_gx, n_gy, pulls, owners, codes, states, velocity,
    inbox, later, rows_in, cols_in, requested,
    states_v, velocity_v, rows_v, cols_v, edge_cols, request, requested_v, requested_s,
    field, edges, halo_rows, halo_cols, extended, supplied, later_v,
    load_sem, send_sem, recv_sem, halo_send, halo_recv, code_send, code_recv,
    brick_send, brick_recv,
):
    gx, gy = lax.axis_index("gx"), lax.axis_index("gy")
    rows, depth = states.shape[1], states.shape[3]
    blocks = rows // BX

    def device(step_x, step_y):
        return (lax.rem(gx + step_x + n_gx, n_gx), lax.rem(gy + step_y + n_gy, n_gy))

    def remote(src, dst, send, recv, step_x, step_y):
        return pltpu.make_async_remote_copy(
            src_ref=src, dst_ref=dst, send_sem=send, recv_sem=recv,
            device_id=device(step_x, step_y), device_id_type=pl.DeviceIdType.MESH,
        )

    peers = [(i, j) for i in (-1, 1) for j in (-1, 0, 1)] + [(0, d) for d in range(1, n_gy)]
    barrier = pltpu.get_barrier_semaphore()
    for peer in peers:
        pl.semaphore_signal(
            barrier, inc=1, device_id=device(*peer), device_id_type=pl.DeviceIdType.MESH
        )
    loads = [
        pltpu.make_async_copy(states, states_v, load_sem.at[0]),
        pltpu.make_async_copy(velocity, velocity_v, load_sem.at[1]),
    ]
    for load in loads:
        load.start()
    peer_row = lax.broadcasted_iota(jnp.int32, request.shape, 0)
    entry = lax.broadcasted_iota(jnp.int32, request.shape, 1)
    lane = lax.broadcasted_iota(jnp.int32, request.shape, 2)
    place = jnp.where(entry < CAP, peer_row * CAP + entry, -1)
    table = jnp.zeros(request.shape, jnp.int32)
    for k in range(blocks):
        triple = jnp.where(
            lane == 0, codes[0, k, 0], jnp.where(lane == 1, codes[1, k, 0], codes[2, k, 0])
        )
        table = jnp.where(place == pulls[k, 0], triple, table)
    request[...] = table
    requested_v[pl.ds(gy, 1)] = request[pl.ds(gy, 1)]
    loads[0].wait()
    for step in range(STEPS):
        edge_cols[0, step] = states_v[step, :, BY - 1, :]
        edge_cols[1, step] = states_v[step, :, 0, :]
    pl.semaphore_wait(barrier, len(peers))

    copies = [
        remote(edge_cols.at[0], cols_v.at[0], send_sem.at[0], recv_sem.at[0], 0, 1),
        remote(edge_cols.at[1], cols_v.at[1], send_sem.at[1], recv_sem.at[1], 0, -1),
        remote(states_v.at[:, rows - 1], rows_v.at[0], send_sem.at[2], recv_sem.at[2], 1, 0),
        remote(states_v.at[:, 0], rows_v.at[1], send_sem.at[3], recv_sem.at[3], -1, 0),
    ]
    for copy in copies:
        copy.start()
    code_copies = []
    for d in range(1, n_gy):
        peer = lax.rem(gy + d, n_gy)
        code_copies.append(
            remote(request.at[peer], requested_v.at[gy], code_send.at[d], code_recv.at[d], 0, d)
        )
    for copy in code_copies:
        copy.start()
    loads[1].wait()
    for copy in copies:
        copy.wait()

    @pl.loop(0, blocks)
    def _(block):
        cells = pl.ds(block * BX, BX)
        terms = []
        for step in range(STEPS):
            parts = gradient(states_v, rows_v, cols_v, step, block, blocks)
            terms.append(
                (
                    velocity_v[0, cells] * parts[0]
                    + velocity_v[1, cells] * parts[1]
                    + velocity_v[2, cells] * parts[2]
                )
                * -STEP_SIZE
            )
        field[cells] = terms[0]
        for side, col in ((0, BY - 1), (1, 0), (2, 1)):
            edges[side, cells] = terms[0][:, col, :]
        later_v[cells] = terms[1]

    plan, _, _ = halo_plan((field, edges), (halo_rows, halo_cols), gy, n_gy)
    copies = [
        remote(src, dst, halo_send.at[i], halo_recv.at[i], step_x, step_y)
        for i, (src, dst, step_x, step_y) in enumerate(plan)
    ]
    for copy in copies:
        copy.start()
    saves = [
        pltpu.make_async_copy(later_v, later, load_sem.at[0]),
        pltpu.make_async_copy(rows_v, rows_in, load_sem.at[1]),
        pltpu.make_async_copy(cols_v, cols_in, load_sem.at[2]),
    ]
    for save in saves:
        save.start()
    for copy in code_copies:
        copy.wait()
    tables = [
        pltpu.make_async_copy(requested_v, requested_s, load_sem.at[3]),
        pltpu.make_async_copy(requested_v, requested, load_sem.at[4]),
    ]
    for copy in tables:
        copy.start()
    for copy in tables:
        copy.wait()
    for copy in copies:
        copy.wait()
    assemble(extended, field, halo_rows, halo_cols)

    def supply(peer):
        for e in range(CAP):
            owner = jnp.maximum(owners[0, 0, peer, e], 0)
            shift, weights = code_weights(
                requested_s[peer, e, 0], requested_s[peer, e, 1], requested_s[peer, e, 2]
            )
            supplied[peer * CAP + e] = pull_brick(
                extended[pl.ds(owner * BX, WIN)], shift, weights
            )

    mine = pl.ds(gy * CAP, CAP)

    def brick_copy(d):
        peer = lax.rem(gy + d, n_gy)
        return remote(
            supplied.at[pl.ds(peer * CAP, CAP)], inbox.at[mine],
            brick_send.at[d], brick_recv.at[d], 0, d,
        )

    @pl.loop(1, n_gy)
    def _(d):
        supply(lax.rem(gy + d, n_gy))
        brick_copy(d).start()

    supply(gy)
    own = pltpu.make_async_copy(supplied.at[mine], inbox.at[mine], load_sem.at[5])
    own.start()
    own.wait()
    for save in saves:
        save.wait()

    @pl.loop(1, n_gy)
    def _(d):
        brick_copy(d).wait()


def supply_call(states, velocity, pull_plan, send_plan, codes):
    n_gx, n_gy = lax.axis_size("gx"), lax.axis_size("gy")
    _, rows, cols, depth = states.shape
    slots = n_gy * CAP
    table = (n_gy, 8, 128)
    smem = pl.BlockSpec(memory_space=pltpu.SMEM)
    any_space = pl.BlockSpec(memory_space=pl.ANY)
    dma = pltpu.SemaphoreType.DMA

    def vmem(*dims):
        return pltpu.VMEM(dims, F32)

    return pl.pallas_call(
        lambda *refs: supply_kernel(n_gx, n_gy, *refs),
        name="supply",
        in_specs=[smem, smem, smem, any_space, any_space],
        out_specs=[any_space] * 5,
        out_shape=[
            shape(slots, BX, BY, depth),
            shape(rows, cols, depth),
            shape(2, STEPS, cols, depth),
            shape(2, STEPS, rows, depth),
            jax.ShapeDtypeStruct(table, jnp.int32),
        ],
        scratch_shapes=[
            vmem(STEPS, rows, cols, depth),
            vmem(3, rows, cols, depth),
            vmem(2, STEPS, cols, depth),
            vmem(2, STEPS, rows, depth),
            vmem(2, STEPS, rows, depth),
            pltpu.VMEM(table, jnp.int32),
            pltpu.VMEM(table, jnp.int32),
            pltpu.SMEM(table, jnp.int32),
            vmem(rows, cols, depth),
            vmem(3, rows, depth),
            vmem(3, cols, depth),
            vmem(3, rows + 16, depth),
            vmem(rows + 3, LANES, depth),
            vmem(slots, BX, BY, depth),
            vmem(rows, cols, depth),
            dma((6,)),
            dma((4,)),
            dma((4,)),
            dma((8,)),
            dma((8,)),
            dma((n_gy,)),
            dma((n_gy,)),
            dma((n_gy,)),
            dma((n_gy,)),
        ],
        compiler_params=pltpu.CompilerParams(
            collective_id=0, has_side_effects=True, vmem_limit_bytes=VMEM_LIMIT
        ),
    )(pull_plan, send_plan, codes, states, velocity)


def tangent_kernel(pulls, inbox, later, field, cols):
    emit_field(inbox[0] + later[...], field, cols)


def fold(total, rows_in, cols_in):
    block, blocks = pl.program_id(0), pl.num_programs(0)
    depth = total.shape[2]
    is_first, is_last = block == 0, block == blocks - 1
    rows = cols_in.shape[1] - 16
    zeros = jnp.zeros((8, depth), F32)
    values = total[...]
    col = lax.broadcasted_iota(jnp.int32, values.shape, 1)
    row = lax.broadcasted_iota(jnp.int32, values.shape, 0)
    values = values + jnp.where(jnp.logical_and(is_last, row == BX - 1), rows_in[0:1], 0.0)
    for i in range(2):
        values = values + jnp.where(
            jnp.logical_and(is_first, row == i), rows_in[1 + i : 2 + i], 0.0
        )
    for side, place in ((0, BY - 1), (1, 0), (2, 1)):
        strip = cols_in[side, pl.ds(8 + block * BX, BX)]
        low = jnp.concatenate([cols_in[side, 0:8], zeros], axis=0)
        high = jnp.concatenate([zeros, cols_in[side, rows + 8 : rows + 16]], axis=0)
        strip = strip + jnp.where(is_first, low, 0.0) + jnp.where(is_last, high, 0.0)
        values = values + jnp.where(col == place, strip[:, None, :], 0.0)
    return values


def outbox_kernel(pulls, total, rows_in, cols_in, adjoint, outbox):
    values = fold(total, rows_in, cols_in)
    adjoint[...] = values
    outbox[0] = values


def force_kernel(
    states, rows_in, cols_in, later_adjoint, total, fold_rows, fold_cols, force
):
    block, blocks = pl.program_id(0), pl.num_programs(0)
    adjoints = [fold(total, fold_rows, fold_cols), later_adjoint[...]]
    scaled = [adjoint * -STEP_SIZE for adjoint in adjoints]
    early = gradient(states, rows_in, cols_in, 0, block, blocks)
    late = gradient(states, rows_in, cols_in, 1, block, blocks)
    for c in range(3):
        force[c] = scaled[1] * late[c] + scaled[0] * early[c]


def whole(dims):
    return pl.BlockSpec(dims, lambda *_: (0,) * len(dims))


def local_call(kernel, name, steps, scalars, in_specs, out_specs, out_shapes, scratch, operands):
    return pl.pallas_call(
        kernel,
        name=name,
        grid_spec=pltpu.PrefetchScalarGridSpec(
            num_scalar_prefetch=len(scalars),
            grid=(steps,),
            in_specs=in_specs,
            out_specs=out_specs,
            scratch_shapes=scratch,
        ),
        out_shape=out_shapes,
        compiler_params=pltpu.CompilerParams(vmem_limit_bytes=VMEM_LIMIT),
    )(*scalars, *operands)


def body(velocity, states, pull_plan, send_plan, codes):
    _, rows, cols, depth = velocity.shape
    assert cols == BY and rows % BX == 0
    bricks = rows // BX
    peers = lax.axis_size("gy")
    slots = peers * CAP
    pulls = pull_plan.reshape(bricks)
    owners = send_plan.reshape(slots)
    inbox, later, state_rows, state_cols, requested = supply_call(
        states, velocity, pull_plan, send_plan, codes
    )
    slot_codes = requested[:, :CAP, :3].reshape(slots * 3)

    block = pl.BlockSpec((BX, BY, depth), lambda k, *_: (k, 0, 0))
    vector_block = pl.BlockSpec((3, BX, BY, depth), lambda k, *_: (0, k, 0, 0))
    edge_block = pl.BlockSpec((3, BX, depth), lambda k, *_: (0, k, 0))
    slot_block = pl.BlockSpec((1, BX, BY, depth), lambda s, *_: (s, 0, 0, 0))
    named_block = pl.BlockSpec((1, BX, BY, depth), lambda k, plan: (plan[k], 0, 0, 0))
    state_specs = [whole(states.shape), whole(state_rows.shape), whole(state_cols.shape)]
    field_shape = shape(rows, cols, depth)
    edge_shape = shape(3, rows, depth)
    margin_shapes = [shape(3, cols, depth), shape(3, rows + 16, depth)]
    margin_specs = [whole(s.shape) for s in margin_shapes]
    field_spec = whole(field_shape.shape)
    slot_shape = shape(slots, BX, BY, depth)
    extended = pltpu.VMEM((rows + 3, LANES, depth), F32)

    field, edges = local_call(
        tangent_kernel, "tangent", bricks, (pulls,), [named_block, block],
        [block, edge_block], [field_shape, edge_shape], [], (inbox, later),
    )
    halo = exchange("exchange_tangent", 3, (field, edges), margin_shapes, halo_plan)
    total, *margins = local_call(
        pull_push_kernel, "pull_push", slots, (owners, slot_codes), [field_spec] + margin_specs,
        [field_spec] + margin_specs, [field_shape] + margin_shapes, [extended, extended],
        (field, *halo),
    )
    margins = exchange("fold_late", 4, margins, margin_shapes, fold_plan)
    late_adjoint, outbox = local_call(
        outbox_kernel, "outbox", bricks, (pulls,), [block] + margin_specs,
        [block, named_block], [field_shape, slot_shape], [], (total, *margins),
    )
    (inbox,) = exchange("exchange_adjoint", 5, (outbox,), [slot_shape], bricks_plan)
    total, *margins = local_call(
        push_kernel, "push", slots, (owners, slot_codes), [slot_block],
        [field_spec] + margin_specs, [field_shape] + margin_shapes, [extended], (inbox,),
    )
    margins = exchange("fold_early", 6, margins, margin_shapes, fold_plan)
    return local_call(
        force_kernel, "force", bricks, (), state_specs + [block, block] + margin_specs,
        vector_block, shape(3, rows, cols, depth), [],
        (states, state_rows, state_cols, late_adjoint, total, *margins),
    )


def solution(mesh):
    return jax.shard_map(
        body,
        mesh=mesh,
        in_specs=(
            P(None, "gx", "gy", None),
            P(None, "gx", "gy", None),
            P("gx", "gy"),
            P("gx", "gy", None, None),
            P(None, "gx", "gy"),
        ),
        out_specs=P(None, "gx", "gy", None),
        check_vma=False,
    )
```

```python
import functools

import jax
import jax.numpy as jnp
from jax import lax
from jax.experimental import pallas as pl
from jax.experimental.pallas import tpu as pltpu
from jax.sharding import PartitionSpec as P

BX = 16
BY = 16
CAP = 2
QF = 8
STEPS = 2
STEP_SIZE = 1.0 / STEPS
WIN = BX + 3
CHUNK = 4
LANES = 24
VMEM_LIMIT = 40 * 1024 * 1024
F32 = jnp.float32


def shape(*dims):
    return jax.ShapeDtypeStruct(dims, F32)


def halo_plan(ins, outs):
    field, cols = ins
    rows_in, cols_in = outs
    rows = field.shape[0]
    main, low, high = pl.ds(8, rows), pl.ds(0, 8), pl.ds(rows + 8, 8)
    first, last = pl.ds(0, 8), pl.ds(rows - 8, 8)
    one, two = pl.ds(0, 1), pl.ds(1, 2)
    remote = [
        (cols.at[one], cols_in.at[one, main], 0, 1),
        (cols.at[two], cols_in.at[two, main], 0, -1),
        (field.at[pl.ds(rows - 1, 1)], rows_in.at[one], 1, 0),
        (field.at[pl.ds(0, 2)], rows_in.at[two], -1, 0),
        (cols.at[one, last], cols_in.at[one, low], 1, 1),
        (cols.at[one, first], cols_in.at[one, high], -1, 1),
        (cols.at[two, last], cols_in.at[two, low], 1, -1),
        (cols.at[two, first], cols_in.at[two, high], -1, -1),
    ]
    return remote


def fold_plan(ins, outs):
    rows_out, cols = ins
    rows_in, cols_in = outs
    rows = cols.shape[1] - 16
    main, low, high = pl.ds(8, rows), pl.ds(0, 8), pl.ds(rows + 8, 8)
    one, two = pl.ds(0, 1), pl.ds(1, 2)
    remote = [
        (cols.at[one, main], cols_in.at[one, main], 0, -1),
        (cols.at[two, main], cols_in.at[two, main], 0, 1),
        (rows_out.at[one], rows_in.at[one], -1, 0),
        (rows_out.at[two], rows_in.at[two], 1, 0),
        (cols.at[one, low], cols_in.at[one, high], -1, -1),
        (cols.at[one, high], cols_in.at[one, low], 1, -1),
        (cols.at[two, low], cols_in.at[two, high], -1, 1),
        (cols.at[two, high], cols_in.at[two, low], 1, 1),
    ]
    return remote


def cubic_weights(f):
    return (
        -f * (f - 1.0) * (f - 2.0) * (1.0 / 6.0),
        (f + 1.0) * (f - 1.0) * (f - 2.0) * 0.5,
        -(f + 1.0) * f * (f - 2.0) * 0.5,
        (f + 1.0) * f * (f - 1.0) * (1.0 / 6.0),
    )


def code_weights(u, v, q):
    depth_shift = lax.shift_right_logical(q, 3)
    fractions = [u, v, jnp.bitwise_and(q, QF - 1)]
    return depth_shift, [cubic_weights(f.astype(F32) * (1.0 / QF)) for f in fractions]


def weighted(weights, terms):
    total = weights[0] * terms[0]
    for weight, term in zip(weights[1:], terms[1:]):
        total = total + weight * term
    return total


def pull_rows(window, shift, weights):
    count, depth = window.shape[0] - 3, window.shape[2]
    rows = weighted(weights[0], [window[r : r + count] for r in range(4)])
    cols = weighted(
        weights[1],
        [(rows if t == 0 else pltpu.roll(rows, LANES - t, 1))[:, :BY] for t in range(4)],
    )
    base = pltpu.roll(cols, lax.rem(depth + 1 - shift, depth), 2)
    return weighted(
        weights[2], [base if m == 0 else pltpu.roll(base, depth - m, 2) for m in range(4)]
    )


def push_rows(values, shift, weights):
    count, _, depth = values.shape
    base = pltpu.roll(values, lax.rem(depth - 1 + shift, depth), 2)
    along = weighted(weights[2], [base if m == 0 else pltpu.roll(base, m, 2) for m in range(4)])
    wide = jnp.concatenate([along, jnp.zeros((count, LANES - BY, depth), F32)], axis=1)
    cols = weighted(weights[1], [wide if t == 0 else pltpu.roll(wide, t, 1) for t in range(4)])
    rows = []
    for i in range(count + 3):
        terms = [cols[i - r] * weights[0][r] for r in range(4) if 0 <= i - r < count]
        rows.append(sum(terms[1:], terms[0])[None])
    return jnp.concatenate(rows, axis=0)


def assemble(extended, field, rows_in, cols_in):
    rows = field.shape[0]
    extended[1 : rows + 1, 1 : BY + 1, :] = field[...]
    extended[0:1, 1 : BY + 1, :] = rows_in[0:1]
    extended[rows + 1 : rows + 3, 1 : BY + 1, :] = rows_in[1:3]
    for col, side in ((0, 0), (BY + 1, 1), (BY + 2, 2)):
        extended[:, col, :] = cols_in[side, 7 : rows + 10, :]


def emit_margins(total, acc, rows_out, cols_out):
    rows = total.shape[0]
    total[...] = acc[1 : rows + 1, 1 : BY + 1, :]
    rows_out[0:1] = acc[0:1, 1 : BY + 1, :]
    rows_out[1:3] = acc[rows + 1 : rows + 3, 1 : BY + 1, :]
    cols_out[...] = jnp.zeros_like(cols_out)
    for col, side in ((0, 0), (BY + 1, 1), (BY + 2, 2)):
        cols_out[side, 7 : rows + 10, :] = acc[:, col, :]


def gradient(states, rows_in, cols_in, step, block, blocks):
    rows, depth = states.shape[1], states.shape[3]
    first = block * BX
    cells = states[step, pl.ds(first, BX)]
    before = states[step, pl.ds(jnp.maximum(first - 1, 0), 1)]
    after = states[step, pl.ds(jnp.minimum(first + BX, rows - 1), 1)]
    before = jnp.where(block == 0, rows_in[0, pl.ds(step, 1)], before)
    after = jnp.where(block == blocks - 1, rows_in[1, pl.ds(step, 1)], after)
    left = cols_in[0, step, pl.ds(first, BX)][:, None, :]
    right = cols_in[1, step, pl.ds(first, BX)][:, None, :]
    col = lax.broadcasted_iota(jnp.int32, cells.shape, 1)
    below = jnp.concatenate([before, cells[:-1]], axis=0)
    above = jnp.concatenate([cells[1:], after], axis=0)
    lower = jnp.where(col == 0, left, pltpu.roll(cells, 1, 1))
    upper = jnp.where(col == BY - 1, right, pltpu.roll(cells, BY - 1, 1))
    return (
        (above - below) * 0.5,
        (upper - lower) * 0.5,
        (pltpu.roll(cells, depth - 1, 2) - pltpu.roll(cells, 1, 2)) * 0.5,
    )


def adjoints_kernel(
    n_gx, n_gy, plan, states, velocity,
    late_out, early_out, rows_out, cols_out,
    states_v, velocity_v, rows_v, cols_v, edge_cols, request, requested_v, requested_s,
    field, edges, halo_rows, halo_cols, extended, supplied, later_v, inbox,
    next_field, next_edges, next_rows, next_cols, running, sums, acc,
    total, late_margin_rows, late_margin_cols, late_fold_rows, late_fold_cols, late,
    outbox, returned, early_margin_rows, early_margin_cols, early_fold_rows, early_fold_cols,
    early, rank, order, sorted_owner, load_sem, send_sem, recv_sem, code_send, code_recv,
    brick_send, brick_recv, margin_send, margin_recv,
):
    gx, gy = lax.axis_index("gx"), lax.axis_index("gy")
    rows, depth = states.shape[1], states.shape[3]
    blocks, slots = rows // BX, n_gy * CAP

    def pull_of(k):
        return plan[k]

    def owner_of(slot):
        return plan[blocks + slot]

    def code_of(c, k):
        return plan[blocks + slots + c * blocks + k]

    def device(step_x, step_y):
        return (lax.rem(gx + step_x + n_gx, n_gx), lax.rem(gy + step_y + n_gy, n_gy))

    def remote(src, dst, send, recv, step_x, step_y):
        return pltpu.make_async_remote_copy(
            src_ref=src, dst_ref=dst, send_sem=send, recv_sem=recv,
            device_id=device(step_x, step_y), device_id_type=pl.DeviceIdType.MESH,
        )

    peers = [(i, j) for i in (-1, 1) for j in (-1, 0, 1)] + [(0, d) for d in range(1, n_gy)]
    barrier = pltpu.get_barrier_semaphore()
    for peer in peers:
        pl.semaphore_signal(
            barrier, inc=1, device_id=device(*peer), device_id_type=pl.DeviceIdType.MESH
        )
    loads = [
        pltpu.make_async_copy(states, states_v, load_sem.at[0]),
        pltpu.make_async_copy(velocity, velocity_v, load_sem.at[1]),
    ]
    for load in loads:
        load.start()
    peer_row = lax.broadcasted_iota(jnp.int32, request.shape, 0)
    entry = lax.broadcasted_iota(jnp.int32, request.shape, 1)
    lane = lax.broadcasted_iota(jnp.int32, request.shape, 2)
    place = jnp.where(entry < CAP, peer_row * CAP + entry, -1)
    table = jnp.zeros(request.shape, jnp.int32)
    for k in range(blocks):
        triple = jnp.where(
            lane == 0, code_of(0, k), jnp.where(lane == 1, code_of(1, k), code_of(2, k))
        )
        table = jnp.where(place == pull_of(k), triple, table)
    request[...] = table
    requested_v[pl.ds(gy, 1)] = request[pl.ds(gy, 1)]
    loads[0].wait()
    for step in range(STEPS):
        edge_cols[0, step] = states_v[step, :, BY - 1, :]
        edge_cols[1, step] = states_v[step, :, 0, :]
    pl.semaphore_wait(barrier, len(peers))

    copies = [
        remote(edge_cols.at[0], cols_v.at[0], send_sem.at[0], recv_sem.at[0], 0, 1),
        remote(edge_cols.at[1], cols_v.at[1], send_sem.at[1], recv_sem.at[1], 0, -1),
        remote(states_v.at[:, rows - 1], rows_v.at[0], send_sem.at[2], recv_sem.at[2], 1, 0),
        remote(states_v.at[:, 0], rows_v.at[1], send_sem.at[3], recv_sem.at[3], -1, 0),
    ]
    for copy in copies:
        copy.start()
    code_copies = []
    for d in range(1, n_gy):
        peer = lax.rem(gy + d, n_gy)
        code_copies.append(
            remote(request.at[peer], requested_v.at[gy], code_send.at[d], code_recv.at[d], 0, d)
        )
    for copy in code_copies:
        copy.start()
    loads[1].wait()
    for copy in copies:
        copy.wait()

    @pl.loop(0, blocks)
    def _(block):
        cells = pl.ds(block * BX, BX)
        terms = []
        for step in range(STEPS):
            parts = gradient(states_v, rows_v, cols_v, step, block, blocks)
            terms.append(
                (
                    velocity_v[0, cells] * parts[0]
                    + velocity_v[1, cells] * parts[1]
                    + velocity_v[2, cells] * parts[2]
                )
                * -STEP_SIZE
            )
        field[cells] = terms[0]
        for side, col in ((0, BY - 1), (1, 0), (2, 1)):
            edges[side, cells] = terms[0][:, col, :]
        later_v[cells] = terms[1]

    def margin_copies(phase, moves):
        copies = [
            remote(src, dst, margin_send.at[phase, i], margin_recv.at[phase, i], step_x, step_y)
            for i, (src, dst, step_x, step_y) in enumerate(moves)
        ]
        for copy in copies:
            copy.start()
        return copies

    copies = margin_copies(0, halo_plan((field, edges), (halo_rows, halo_cols)))
    saves = [
        pltpu.make_async_copy(rows_v, rows_out, load_sem.at[0]),
        pltpu.make_async_copy(cols_v, cols_out, load_sem.at[1]),
    ]
    for save in saves:
        save.start()
    for copy in code_copies:
        copy.wait()
    table_copy = pltpu.make_async_copy(requested_v, requested_s, load_sem.at[2])
    table_copy.start()
    table_copy.wait()
    for copy in copies:
        copy.wait()
    assemble(extended, field, halo_rows, halo_cols)

    def codes_of(slot):
        peer, e = lax.shift_right_logical(slot, 1), jnp.bitwise_and(slot, 1)
        return code_weights(*[requested_s[peer, e, c] for c in range(3)])

    def supply(peer, target):
        for e in range(CAP):
            slot = peer * CAP + e
            first = jnp.maximum(owner_of(slot), 0) * BX
            shift, weights = codes_of(slot)
            for row in range(0, BX, CHUNK):
                target[slot, row : row + CHUNK] = pull_rows(
                    extended[pl.ds(first + row, CHUNK + 3)], shift, weights
                )

    def brick_copy(phase, d, source, target):
        peer = lax.rem(gy + d, n_gy)
        return remote(
            source.at[pl.ds(peer * CAP, CAP)], target.at[pl.ds(gy * CAP, CAP)],
            brick_send.at[phase, d], brick_recv.at[phase, d], 0, d,
        )

    @pl.loop(1, n_gy)
    def _(d):
        supply(lax.rem(gy + d, n_gy), supplied)
        brick_copy(0, d, supplied, inbox).start()

    supply(gy, inbox)

    @pl.loop(0, slots)
    def _(s):
        mine = owner_of(s)

        def ahead(t, count):
            other = owner_of(t)
            before = jnp.logical_or(other < mine, jnp.logical_and(other == mine, t < s))
            return count + jnp.where(before, 1, 0)

        rank[s] = lax.fori_loop(0, slots, ahead, 0)

    @pl.loop(0, slots)
    def _(j):
        found = lax.fori_loop(0, slots, lambda t, at: jnp.where(rank[t] == j, t, at), 0)
        order[j] = found
        sorted_owner[j] = owner_of(found)

    for save in saves:
        save.wait()

    @pl.loop(1, n_gy)
    def _(d):
        brick_copy(0, d, supplied, inbox).wait()

    @pl.loop(0, blocks)
    def _(block):
        cells = pl.ds(block * BX, BX)
        values = inbox[pull_of(block)] + later_v[cells]
        next_field[cells] = values
        for side, col in ((0, BY - 1), (1, 0), (2, 1)):
            next_edges[side, cells] = values[:, col, :]

    for copy in margin_copies(1, halo_plan((next_field, next_edges), (next_rows, next_cols))):
        copy.wait()
    assemble(extended, next_field, next_rows, next_cols)

    def accumulate(values_of):
        running[...] = jnp.zeros_like(running)

        @pl.loop(0, slots)
        def _(j):
            slot, owner = order[j], sorted_owner[j]
            previous = sorted_owner[jnp.maximum(j - 1, 0)]
            running[...] = jnp.where(owner == previous, running[...], 0.0)
            shift, weights = codes_of(slot)
            first = jnp.maximum(owner, 0) * BX
            for row in range(0, BX, CHUNK):
                part = push_rows(values_of(slot, first, row, shift, weights), shift, weights)
                running[row : row + CHUNK + 3] = running[row : row + CHUNK + 3] + part
            sums[j] = running[...]

        acc[...] = jnp.zeros_like(acc)

        @pl.loop(0, blocks)
        def _(k):
            def at_most(t, count):
                return count + jnp.where(sorted_owner[t] <= k, 1, 0)

            last = jnp.maximum(lax.fori_loop(0, slots, at_most, 0) - 1, 0)
            window = pl.ds(k * BX, WIN)
            acc[window] = acc[window] + jnp.where(sorted_owner[last] == k, sums[last], 0.0)

    def fold_all(fold_rows, fold_cols, target):
        @pl.loop(0, blocks)
        def _(block):
            cells = pl.ds(block * BX, BX)
            target[cells] = fold(total[cells], fold_rows, fold_cols, block, blocks)

    def pulled(slot, first, row, shift, weights):
        return pull_rows(extended[pl.ds(first + row, CHUNK + 3)], shift, weights)

    accumulate(pulled)
    emit_margins(total, acc, late_margin_rows, late_margin_cols)
    moves = fold_plan((late_margin_rows, late_margin_cols), (late_fold_rows, late_fold_cols))
    for copy in margin_copies(2, moves):
        copy.wait()
    fold_all(late_fold_rows, late_fold_cols, late)
    late_save = pltpu.make_async_copy(late, late_out, load_sem.at[3])
    late_save.start()

    def fill(peer, target):
        for e in range(CAP):
            slot = peer * CAP + e
            brick = 0
            for k in range(1, blocks):
                brick = jnp.where(pull_of(k) == slot, k, brick)
            target[slot] = late[pl.ds(brick * BX, BX)]

    @pl.loop(1, n_gy)
    def _(d):
        fill(lax.rem(gy + d, n_gy), outbox)
        brick_copy(1, d, outbox, returned).start()

    fill(gy, returned)
    late_save.wait()

    @pl.loop(1, n_gy)
    def _(d):
        brick_copy(1, d, outbox, returned).wait()

    accumulate(lambda slot, first, row, shift, weights: returned[slot, row : row + CHUNK])
    emit_margins(total, acc, early_margin_rows, early_margin_cols)
    moves = fold_plan((early_margin_rows, early_margin_cols), (early_fold_rows, early_fold_cols))
    for copy in margin_copies(3, moves):
        copy.wait()
    fold_all(early_fold_rows, early_fold_cols, early)
    early_save = pltpu.make_async_copy(early, early_out, load_sem.at[4])
    early_save.start()
    early_save.wait()


def adjoints_call(states, velocity, plan):
    n_gx, n_gy = lax.axis_size("gx"), lax.axis_size("gy")
    _, rows, cols, depth = states.shape
    slots = n_gy * CAP
    table = (n_gy, 8, 128)
    hbm = pl.BlockSpec(memory_space=pltpu.HBM)
    dma = pltpu.SemaphoreType.DMA

    def vmem(*dims):
        return pltpu.VMEM(dims, F32)

    field = vmem(rows, cols, depth)
    edges = vmem(3, rows, depth)
    margin_rows, margin_cols = vmem(3, cols, depth), vmem(3, rows + 16, depth)
    extended = vmem(rows + 3, LANES, depth)
    bricks = vmem(slots, BX, BY, depth)
    margins = [margin_rows, margin_cols]
    return pl.pallas_call(
        lambda *refs: adjoints_kernel(n_gx, n_gy, *refs),
        name="adjoints",
        in_specs=[pl.BlockSpec(memory_space=pltpu.SMEM), hbm, hbm],
        out_specs=[hbm] * 4,
        out_shape=[
            shape(rows, cols, depth),
            shape(rows, cols, depth),
            shape(2, STEPS, cols, depth),
            shape(2, STEPS, rows, depth),
        ],
        scratch_shapes=[
            vmem(STEPS, rows, cols, depth),
            vmem(3, rows, cols, depth),
            vmem(2, STEPS, cols, depth),
            vmem(2, STEPS, rows, depth),
            vmem(2, STEPS, rows, depth),
            pltpu.VMEM(table, jnp.int32),
            pltpu.VMEM(table, jnp.int32),
            pltpu.SMEM(table, jnp.int32),
            field,
            edges,
            *margins,
            extended,
            bricks,
            field,
            bricks,
            field,
            edges,
            *margins,
            vmem(WIN, LANES, depth),
            vmem(slots, WIN, LANES, depth),
            extended,
            field,
            *margins,
            *margins,
            field,
            bricks,
            bricks,
            *margins,
            *margins,
            field,
            pltpu.SMEM((slots,), jnp.int32),
            pltpu.SMEM((slots,), jnp.int32),
            pltpu.SMEM((slots,), jnp.int32),
            dma((5,)),
            dma((4,)),
            dma((4,)),
            dma((n_gy,)),
            dma((n_gy,)),
            dma((2, n_gy)),
            dma((2, n_gy)),
            dma((4, 8)),
            dma((4, 8)),
        ],
        compiler_params=pltpu.CompilerParams(
            collective_id=0, has_side_effects=True, vmem_limit_bytes=VMEM_LIMIT
        ),
    )(plan, states, velocity)


def fold(values, rows_in, cols_in, block, blocks):
    depth = values.shape[2]
    is_first, is_last = block == 0, block == blocks - 1
    rows = cols_in.shape[1] - 16
    zeros = jnp.zeros((8, depth), F32)
    col = lax.broadcasted_iota(jnp.int32, values.shape, 1)
    row = lax.broadcasted_iota(jnp.int32, values.shape, 0)
    values = values + jnp.where(jnp.logical_and(is_last, row == BX - 1), rows_in[0:1], 0.0)
    for i in range(2):
        values = values + jnp.where(
            jnp.logical_and(is_first, row == i), rows_in[1 + i : 2 + i], 0.0
        )
    for side, place in ((0, BY - 1), (1, 0), (2, 1)):
        strip = cols_in[side, pl.ds(8 + block * BX, BX)]
        low = jnp.concatenate([cols_in[side, 0:8], zeros], axis=0)
        high = jnp.concatenate([zeros, cols_in[side, rows + 8 : rows + 16]], axis=0)
        strip = strip + jnp.where(is_first, low, 0.0) + jnp.where(is_last, high, 0.0)
        values = values + jnp.where(col == place, strip[:, None, :], 0.0)
    return values


def force_kernel(states, rows_in, cols_in, late_adjoint, early_adjoint, force):
    block, blocks = pl.program_id(0), pl.num_programs(0)
    scaled = [early_adjoint[...] * -STEP_SIZE, late_adjoint[...] * -STEP_SIZE]
    early = gradient(states, rows_in, cols_in, 0, block, blocks)
    late = gradient(states, rows_in, cols_in, 1, block, blocks)
    for c in range(3):
        force[c] = scaled[1] * late[c] + scaled[0] * early[c]


def whole(dims):
    return pl.BlockSpec(dims, lambda *_: (0,) * len(dims))


def body(velocity, states, pull_plan, send_plan, codes):
    _, rows, cols, depth = velocity.shape
    assert cols == BY and rows % BX == 0
    plan = jnp.concatenate([pull_plan.reshape(-1), send_plan.reshape(-1), codes.reshape(-1)])
    late_adjoint, early_adjoint, state_rows, state_cols = adjoints_call(states, velocity, plan)
    block = pl.BlockSpec((BX, BY, depth), lambda k: (k, 0, 0))
    return pl.pallas_call(
        force_kernel,
        name="force",
        grid=(rows // BX,),
        in_specs=[whole(states.shape), whole(state_rows.shape), whole(state_cols.shape)]
        + [block, block],
        out_specs=pl.BlockSpec((3, BX, BY, depth), lambda k: (0, k, 0, 0)),
        out_shape=shape(3, rows, cols, depth),
        compiler_params=pltpu.CompilerParams(vmem_limit_bytes=VMEM_LIMIT),
    )(states, state_rows, state_cols, late_adjoint, early_adjoint)


def solution(mesh):
    return jax.shard_map(
        body,
        mesh=mesh,
        in_specs=(
            P(None, "gx", "gy", None),
            P(None, "gx", "gy", None),
            P("gx", "gy"),
            P("gx", "gy", None, None),
            P(None, "gx", "gy"),
        ),
        out_specs=P(None, "gx", "gy", None),
        check_vma=False,
    )
```

```python
import functools

import jax
import jax.numpy as jnp
from jax import lax
from jax.experimental import pallas as pl
from jax.experimental.pallas import tpu as pltpu
from jax.sharding import PartitionSpec as P

BX = 16
BY = 16
CAP = 2
QF = 8
STEPS = 2
STEP_SIZE = 1.0 / STEPS
WIN = BX + 3
CHUNK = 4
LANES = 24
VMEM_LIMIT = 60 * 1024 * 1024
F32 = jnp.float32


def shape(*dims):
    return jax.ShapeDtypeStruct(dims, F32)


def halo_plan(ins, outs):
    field, cols = ins
    rows_in, cols_in = outs
    rows = field.shape[0]
    main, low, high = pl.ds(8, rows), pl.ds(0, 8), pl.ds(rows + 8, 8)
    first, last = pl.ds(0, 8), pl.ds(rows - 8, 8)
    one, two = pl.ds(0, 1), pl.ds(1, 2)
    remote = [
        (cols.at[one], cols_in.at[one, main], 0, 1),
        (cols.at[two], cols_in.at[two, main], 0, -1),
        (field.at[pl.ds(rows - 1, 1)], rows_in.at[one], 1, 0),
        (field.at[pl.ds(0, 2)], rows_in.at[two], -1, 0),
        (cols.at[one, last], cols_in.at[one, low], 1, 1),
        (cols.at[one, first], cols_in.at[one, high], -1, 1),
        (cols.at[two, last], cols_in.at[two, low], 1, -1),
        (cols.at[two, first], cols_in.at[two, high], -1, -1),
    ]
    return remote


def fold_plan(ins, outs):
    rows_out, cols = ins
    rows_in, cols_in = outs
    rows = cols.shape[1] - 16
    main, low, high = pl.ds(8, rows), pl.ds(0, 8), pl.ds(rows + 8, 8)
    one, two = pl.ds(0, 1), pl.ds(1, 2)
    remote = [
        (cols.at[one, main], cols_in.at[one, main], 0, -1),
        (cols.at[two, main], cols_in.at[two, main], 0, 1),
        (rows_out.at[one], rows_in.at[one], -1, 0),
        (rows_out.at[two], rows_in.at[two], 1, 0),
        (cols.at[one, low], cols_in.at[one, high], -1, -1),
        (cols.at[one, high], cols_in.at[one, low], 1, -1),
        (cols.at[two, low], cols_in.at[two, high], -1, 1),
        (cols.at[two, high], cols_in.at[two, low], 1, 1),
    ]
    return remote


def cubic_weights(f):
    return (
        -f * (f - 1.0) * (f - 2.0) * (1.0 / 6.0),
        (f + 1.0) * (f - 1.0) * (f - 2.0) * 0.5,
        -(f + 1.0) * f * (f - 2.0) * 0.5,
        (f + 1.0) * f * (f - 1.0) * (1.0 / 6.0),
    )


def code_weights(u, v, q):
    depth_shift = lax.shift_right_logical(q, 3)
    fractions = [u, v, jnp.bitwise_and(q, QF - 1)]
    return depth_shift, [cubic_weights(f.astype(F32) * (1.0 / QF)) for f in fractions]


def weighted(weights, terms):
    total = weights[0] * terms[0]
    for weight, term in zip(weights[1:], terms[1:]):
        total = total + weight * term
    return total


def pull_sides(window, weights):
    count = window.shape[0] - 3
    rows = weighted(weights[0], [window[r : r + count] for r in range(4)])
    return weighted(
        weights[1],
        [(rows if t == 0 else pltpu.roll(rows, LANES - t, 1))[:, :BY] for t in range(4)],
    )


def pull_depth(values, shift, weights):
    depth = values.shape[2]
    base = pltpu.roll(values, lax.rem(depth + 1 - shift, depth), 2)
    return weighted(
        weights[2], [base if m == 0 else pltpu.roll(base, depth - m, 2) for m in range(4)]
    )


def push_depth(values, shift, weights):
    depth = values.shape[2]
    base = pltpu.roll(values, lax.rem(depth - 1 + shift, depth), 2)
    return weighted(weights[2], [base if m == 0 else pltpu.roll(base, m, 2) for m in range(4)])


def pull_push_depth(values, weights):
    depth = values.shape[2]
    w = weights[2]
    total = (w[0] * w[0] + w[1] * w[1] + w[2] * w[2] + w[3] * w[3]) * values
    for lag in range(1, 4):
        tap = w[0] * w[lag]
        for m in range(1, 4 - lag):
            tap = tap + w[m] * w[m + lag]
        total = total + tap * (pltpu.roll(values, lag, 2) + pltpu.roll(values, depth - lag, 2))
    return total


def push_sides(window, values_of, weights):
    carry = None
    for first in range(0, BX, CHUNK):
        values = values_of(first)
        depth = values.shape[2]
        wide = jnp.concatenate([values, jnp.zeros((CHUNK, LANES - BY, depth), F32)], axis=1)
        cols = weighted(weights[1], [wide if t == 0 else pltpu.roll(wide, t, 1) for t in range(4)])
        rows = []
        for i in range(CHUNK + 3):
            terms = [cols[i - r] * weights[0][r] for r in range(4) if 0 <= i - r < CHUNK]
            if carry is not None and i < 3:
                terms.append(carry[i])
            rows.append(sum(terms[1:], terms[0]))
        for i in range(CHUNK):
            window[first + i] = rows[i]
        carry = rows[CHUNK:]
    for i in range(3):
        window[BX + i] = carry[i]


def assemble(extended, field, rows_in, cols_in):
    rows = field.shape[0]
    extended[1 : rows + 1, 1 : BY + 1, :] = field[...]
    extended[0:1, 1 : BY + 1, :] = rows_in[0:1]
    extended[rows + 1 : rows + 3, 1 : BY + 1, :] = rows_in[1:3]
    for col, side in ((0, 0), (BY + 1, 1), (BY + 2, 2)):
        extended[:, col, :] = cols_in[side, 7 : rows + 10, :]


def emit_margins(total, acc, rows_out, cols_out):
    rows = total.shape[0]
    total[...] = acc[1 : rows + 1, 1 : BY + 1, :]
    rows_out[0:1] = acc[0:1, 1 : BY + 1, :]
    rows_out[1:3] = acc[rows + 1 : rows + 3, 1 : BY + 1, :]
    cols_out[...] = jnp.zeros_like(cols_out)
    for col, side in ((0, 0), (BY + 1, 1), (BY + 2, 2)):
        cols_out[side, 7 : rows + 10, :] = acc[:, col, :]


def gradient(states, rows_in, cols_in, step, block, blocks):
    rows, depth = states.shape[1], states.shape[3]
    first = block * BX
    cells = states[step, pl.ds(first, BX)]
    before = states[step, pl.ds(jnp.maximum(first - 1, 0), 1)]
    after = states[step, pl.ds(jnp.minimum(first + BX, rows - 1), 1)]
    before = jnp.where(block == 0, rows_in[0, pl.ds(step, 1)], before)
    after = jnp.where(block == blocks - 1, rows_in[1, pl.ds(step, 1)], after)
    left = cols_in[0, step, pl.ds(first, BX)][:, None, :]
    right = cols_in[1, step, pl.ds(first, BX)][:, None, :]
    col = lax.broadcasted_iota(jnp.int32, cells.shape, 1)
    below = jnp.concatenate([before, cells[:-1]], axis=0)
    above = jnp.concatenate([cells[1:], after], axis=0)
    lower = jnp.where(col == 0, left, pltpu.roll(cells, 1, 1))
    upper = jnp.where(col == BY - 1, right, pltpu.roll(cells, BY - 1, 1))
    return (
        (above - below) * 0.5,
        (upper - lower) * 0.5,
        (pltpu.roll(cells, depth - 1, 2) - pltpu.roll(cells, 1, 2)) * 0.5,
    )


def adjoints_kernel(
    n_gx, n_gy, plan, states, velocity,
    force,
    states_v, velocity_v, rows_v, cols_v, edge_cols, request, requested_v, requested_s,
    field, edges, halo_rows, halo_cols, extended, supplied, later_v, inbox,
    next_field, next_edges, next_rows, next_cols, pushed, sums, acc,
    total, late_margin_rows, late_margin_cols, late_fold_rows, late_fold_cols, late,
    outbox, returned, early_margin_rows, early_margin_cols, early_fold_rows, early_fold_cols,
    early_slopes, rank, order, sorted_owner, save_sem, load_sem, send_sem, recv_sem, code_send, code_recv,
    brick_send, brick_recv, margin_send, margin_recv,
):
    gx, gy = lax.axis_index("gx"), lax.axis_index("gy")
    rows, depth = states.shape[1], states.shape[3]
    blocks, slots = rows // BX, n_gy * CAP

    def pull_of(k):
        return plan[k]

    def owner_of(slot):
        return plan[blocks + slot]

    def code_of(c, k):
        return plan[blocks + slots + c * blocks + k]

    def device(step_x, step_y):
        return (lax.rem(gx + step_x + n_gx, n_gx), lax.rem(gy + step_y + n_gy, n_gy))

    def remote(src, dst, send, recv, step_x, step_y):
        return pltpu.make_async_remote_copy(
            src_ref=src, dst_ref=dst, send_sem=send, recv_sem=recv,
            device_id=device(step_x, step_y), device_id_type=pl.DeviceIdType.MESH,
        )

    peers = [(i, j) for i in (-1, 1) for j in (-1, 0, 1)] + [(0, d) for d in range(1, n_gy)]
    barrier = pltpu.get_barrier_semaphore()
    for peer in peers:
        pl.semaphore_signal(
            barrier, inc=1, device_id=device(*peer), device_id_type=pl.DeviceIdType.MESH
        )
    loads = [
        pltpu.make_async_copy(states, states_v, load_sem.at[0]),
        pltpu.make_async_copy(velocity, velocity_v, load_sem.at[1]),
    ]
    for load in loads:
        load.start()
    peer_row = lax.broadcasted_iota(jnp.int32, request.shape, 0)
    entry = lax.broadcasted_iota(jnp.int32, request.shape, 1)
    lane = lax.broadcasted_iota(jnp.int32, request.shape, 2)
    place = jnp.where(entry < CAP, peer_row * CAP + entry, -1)
    table = jnp.zeros(request.shape, jnp.int32)
    for k in range(blocks):
        triple = jnp.where(
            lane == 0, code_of(0, k), jnp.where(lane == 1, code_of(1, k), code_of(2, k))
        )
        table = jnp.where(place == pull_of(k), triple, table)
    request[...] = table
    requested_v[pl.ds(gy, 1)] = request[pl.ds(gy, 1)]
    loads[0].wait()
    for step in range(STEPS):
        edge_cols[0, step] = states_v[step, :, BY - 1, :]
        edge_cols[1, step] = states_v[step, :, 0, :]
    pl.semaphore_wait(barrier, len(peers))

    copies = [
        remote(edge_cols.at[0], cols_v.at[0], send_sem.at[0], recv_sem.at[0], 0, 1),
        remote(edge_cols.at[1], cols_v.at[1], send_sem.at[1], recv_sem.at[1], 0, -1),
        remote(states_v.at[:, rows - 1], rows_v.at[0], send_sem.at[2], recv_sem.at[2], 1, 0),
        remote(states_v.at[:, 0], rows_v.at[1], send_sem.at[3], recv_sem.at[3], -1, 0),
    ]
    for copy in copies:
        copy.start()
    code_copies = []
    for d in range(1, n_gy):
        peer = lax.rem(gy + d, n_gy)
        code_copies.append(
            remote(request.at[peer], requested_v.at[gy], code_send.at[d], code_recv.at[d], 0, d)
        )
    for copy in code_copies:
        copy.start()
    loads[1].wait()
    for copy in copies:
        copy.wait()

    @pl.loop(0, blocks)
    def _(block):
        cells = pl.ds(block * BX, BX)
        terms = []
        for step in range(STEPS):
            parts = gradient(states_v, rows_v, cols_v, step, block, blocks)
            terms.append(
                (
                    velocity_v[0, cells] * parts[0]
                    + velocity_v[1, cells] * parts[1]
                    + velocity_v[2, cells] * parts[2]
                )
                * -STEP_SIZE
            )
        field[cells] = terms[0]
        for side, col in ((0, BY - 1), (1, 0), (2, 1)):
            edges[side, cells] = terms[0][:, col, :]
        later_v[cells] = terms[1]

    def margin_copies(phase, moves):
        copies = [
            remote(src, dst, margin_send.at[phase, i], margin_recv.at[phase, i], step_x, step_y)
            for i, (src, dst, step_x, step_y) in enumerate(moves)
        ]
        for copy in copies:
            copy.start()
        return copies

    copies = margin_copies(0, halo_plan((field, edges), (halo_rows, halo_cols)))
    for copy in code_copies:
        copy.wait()
    table_copy = pltpu.make_async_copy(requested_v, requested_s, load_sem.at[2])
    table_copy.start()
    table_copy.wait()
    for copy in copies:
        copy.wait()
    assemble(extended, field, halo_rows, halo_cols)

    def codes_of(slot):
        peer, e = lax.shift_right_logical(slot, 1), jnp.bitwise_and(slot, 1)
        return code_weights(*[requested_s[peer, e, c] for c in range(3)])

    def supply(peer, target):
        for e in range(CAP):
            slot = peer * CAP + e
            first = jnp.maximum(owner_of(slot), 0) * BX
            shift, weights = codes_of(slot)
            for row in range(0, BX, CHUNK):
                sides = pull_sides(extended[pl.ds(first + row, CHUNK + 3)], weights)
                target[slot, row : row + CHUNK] = pull_depth(sides, shift, weights)

    def brick_copy(phase, d, source, target):
        peer = lax.rem(gy + d, n_gy)
        return remote(
            source.at[pl.ds(peer * CAP, CAP)], target.at[pl.ds(gy * CAP, CAP)],
            brick_send.at[phase, d], brick_recv.at[phase, d], 0, d,
        )

    @pl.loop(1, n_gy)
    def _(d):
        supply(lax.rem(gy + d, n_gy), supplied)
        brick_copy(0, d, supplied, inbox).start()

    supply(gy, inbox)

    @pl.loop(0, slots)
    def _(s):
        mine = owner_of(s)

        def ahead(t, count):
            other = owner_of(t)
            before = jnp.logical_or(other < mine, jnp.logical_and(other == mine, t < s))
            return count + jnp.where(before, 1, 0)

        rank[s] = lax.fori_loop(0, slots, ahead, 0)

    @pl.loop(0, slots)
    def _(j):
        found = lax.fori_loop(0, slots, lambda t, at: jnp.where(rank[t] == j, t, at), 0)
        order[j] = found
        sorted_owner[j] = owner_of(found)

    @pl.loop(1, n_gy)
    def _(d):
        brick_copy(0, d, supplied, inbox).wait()

    @pl.loop(0, blocks)
    def _(block):
        cells = pl.ds(block * BX, BX)
        values = inbox[pull_of(block)] + later_v[cells]
        next_field[cells] = values
        for side, col in ((0, BY - 1), (1, 0), (2, 1)):
            next_edges[side, cells] = values[:, col, :]

    for copy in margin_copies(1, halo_plan((next_field, next_edges), (next_rows, next_cols))):
        copy.wait()
    assemble(extended, next_field, next_rows, next_cols)

    def accumulate():
        sums[0] = jnp.zeros(sums.shape[1:], F32)

        @pl.loop(0, slots)
        def _(j):
            before = jnp.maximum(j - 1, 0)
            same = sorted_owner[j] == sorted_owner[before]
            sums[j] = jnp.where(same, sums[before], 0.0) + pushed[order[j]]

        acc[...] = jnp.zeros_like(acc)

        @pl.loop(0, blocks)
        def _(k):
            def at_most(t, count):
                return count + jnp.where(sorted_owner[t] <= k, 1, 0)

            last = jnp.maximum(lax.fori_loop(0, slots, at_most, 0) - 1, 0)
            window = pl.ds(k * BX, WIN)
            acc[window] = acc[window] + jnp.where(sorted_owner[last] == k, sums[last], 0.0)

    def fold_all(fold_rows, fold_cols, target):
        @pl.loop(0, blocks)
        def _(block):
            cells = pl.ds(block * BX, BX)
            target[cells] = fold(total[cells], fold_rows, fold_cols, block, blocks)

    @pl.loop(0, slots)
    def _(slot):
        first = jnp.maximum(owner_of(slot), 0) * BX
        _, weights = codes_of(slot)

        def values_of(row):
            sides = pull_sides(extended[pl.ds(first + row, CHUNK + 3)], weights)
            return pull_push_depth(sides, weights)

        push_sides(pushed.at[slot], values_of, weights)

    accumulate()
    emit_margins(total, acc, late_margin_rows, late_margin_cols)
    moves = fold_plan((late_margin_rows, late_margin_cols), (late_fold_rows, late_fold_cols))
    for copy in margin_copies(2, moves):
        copy.wait()
    fold_all(late_fold_rows, late_fold_cols, late)
    def fill(peer, target):
        for e in range(CAP):
            slot = peer * CAP + e
            brick = 0
            for k in range(1, blocks):
                brick = jnp.where(pull_of(k) == slot, k, brick)
            target[slot] = late[pl.ds(brick * BX, BX)]

    @pl.loop(1, n_gy)
    def _(d):
        fill(lax.rem(gy + d, n_gy), outbox)
        brick_copy(1, d, outbox, returned).start()

    fill(gy, returned)

    @pl.loop(0, blocks)
    def _(block):
        cells = pl.ds(block * BX, BX)
        scaled = late[cells] * -STEP_SIZE
        parts = gradient(states_v, rows_v, cols_v, 1, block, blocks)
        slopes = gradient(states_v, rows_v, cols_v, 0, block, blocks)
        for c in range(3):
            velocity_v[c, cells] = scaled * parts[c]
            early_slopes[c, cells] = slopes[c]

    def push(peer):
        for e in range(CAP):
            slot = peer * CAP + e
            shift, weights = codes_of(slot)
            push_sides(
                pushed.at[slot],
                lambda row: push_depth(returned[slot, row : row + CHUNK], shift, weights),
                weights,
            )

    push(gy)

    @pl.loop(1, n_gy)
    def _(d):
        brick_copy(1, d, outbox, returned).wait()
        push(lax.rem(gy + n_gy - d, n_gy))

    accumulate()
    emit_margins(total, acc, early_margin_rows, early_margin_cols)
    moves = fold_plan((early_margin_rows, early_margin_cols), (early_fold_rows, early_fold_cols))
    for copy in margin_copies(3, moves):
        copy.wait()

    def save(block):
        cells = pl.ds(block * BX, BX)
        return pltpu.make_async_copy(
            velocity_v.at[:, cells], force.at[:, cells], save_sem.at[block]
        )

    @pl.loop(0, blocks)
    def _(block):
        cells = pl.ds(block * BX, BX)
        early = fold(total[cells], early_fold_rows, early_fold_cols, block, blocks)
        scaled = early * -STEP_SIZE
        for c in range(3):
            velocity_v[c, cells] = velocity_v[c, cells] + scaled * early_slopes[c, cells]
        save(block).start()

    @pl.loop(0, blocks)
    def _(block):
        save(block).wait()


def adjoints_call(states, velocity, plan):
    n_gx, n_gy = lax.axis_size("gx"), lax.axis_size("gy")
    _, rows, cols, depth = states.shape
    slots = n_gy * CAP
    table = (n_gy, 8, 128)
    hbm = pl.BlockSpec(memory_space=pltpu.HBM)
    dma = pltpu.SemaphoreType.DMA

    def vmem(*dims):
        return pltpu.VMEM(dims, F32)

    field = vmem(rows, cols, depth)
    edges = vmem(3, rows, depth)
    margin_rows, margin_cols = vmem(3, cols, depth), vmem(3, rows + 16, depth)
    extended = vmem(rows + 3, LANES, depth)
    bricks = vmem(slots, BX, BY, depth)
    margins = [margin_rows, margin_cols]
    return pl.pallas_call(
        lambda *refs: adjoints_kernel(n_gx, n_gy, *refs),
        name="adjoints",
        in_specs=[pl.BlockSpec(memory_space=pltpu.SMEM), hbm, hbm],
        out_specs=hbm,
        out_shape=shape(3, rows, cols, depth),
        scratch_shapes=[
            vmem(STEPS, rows, cols, depth),
            vmem(3, rows, cols, depth),
            vmem(2, STEPS, cols, depth),
            vmem(2, STEPS, rows, depth),
            vmem(2, STEPS, rows, depth),
            pltpu.VMEM(table, jnp.int32),
            pltpu.VMEM(table, jnp.int32),
            pltpu.SMEM(table, jnp.int32),
            field,
            edges,
            *margins,
            extended,
            bricks,
            field,
            bricks,
            field,
            edges,
            *margins,
            vmem(slots, WIN, LANES, depth),
            vmem(slots, WIN, LANES, depth),
            extended,
            field,
            *margins,
            *margins,
            field,
            bricks,
            bricks,
            *margins,
            *margins,
            vmem(3, rows, cols, depth),
            pltpu.SMEM((slots,), jnp.int32),
            pltpu.SMEM((slots,), jnp.int32),
            pltpu.SMEM((slots,), jnp.int32),
            dma((rows // BX,)),
            dma((3,)),
            dma((4,)),
            dma((4,)),
            dma((n_gy,)),
            dma((n_gy,)),
            dma((2, n_gy)),
            dma((2, n_gy)),
            dma((4, 8)),
            dma((4, 8)),
        ],
        compiler_params=pltpu.CompilerParams(
            collective_id=0, has_side_effects=True, vmem_limit_bytes=VMEM_LIMIT
        ),
    )(plan, states, velocity)


def fold(values, rows_in, cols_in, block, blocks):
    depth = values.shape[2]
    is_first, is_last = block == 0, block == blocks - 1
    rows = cols_in.shape[1] - 16
    zeros = jnp.zeros((8, depth), F32)
    col = lax.broadcasted_iota(jnp.int32, values.shape, 1)
    row = lax.broadcasted_iota(jnp.int32, values.shape, 0)
    values = values + jnp.where(jnp.logical_and(is_last, row == BX - 1), rows_in[0:1], 0.0)
    for i in range(2):
        values = values + jnp.where(
            jnp.logical_and(is_first, row == i), rows_in[1 + i : 2 + i], 0.0
        )
    for side, place in ((0, BY - 1), (1, 0), (2, 1)):
        strip = cols_in[side, pl.ds(8 + block * BX, BX)]
        low = jnp.concatenate([cols_in[side, 0:8], zeros], axis=0)
        high = jnp.concatenate([zeros, cols_in[side, rows + 8 : rows + 16]], axis=0)
        strip = strip + jnp.where(is_first, low, 0.0) + jnp.where(is_last, high, 0.0)
        values = values + jnp.where(col == place, strip[:, None, :], 0.0)
    return values


def body(velocity, states, pull_plan, send_plan, codes):
    _, rows, cols, depth = velocity.shape
    assert cols == BY and rows % BX == 0
    plan = jnp.concatenate([pull_plan.reshape(-1), send_plan.reshape(-1), codes.reshape(-1)])
    return adjoints_call(states, velocity, plan)


def solution(mesh):
    return jax.shard_map(
        body,
        mesh=mesh,
        in_specs=(
            P(None, "gx", "gy", None),
            P(None, "gx", "gy", None),
            P("gx", "gy"),
            P("gx", "gy", None, None),
            P(None, "gx", "gy"),
        ),
        out_specs=P(None, "gx", "gy", None),
        check_vma=False,
    )
```

```python
import functools

import jax
import jax.numpy as jnp
from jax import lax
from jax.experimental import pallas as pl
from jax.experimental.pallas import tpu as pltpu
from jax.sharding import PartitionSpec as P

BX = 16
BY = 16
CAP = 2
QF = 8
STEPS = 2
STEP_SIZE = 1.0 / STEPS
WIN = BX + 3
CHUNK = 4
LANES = 24
VMEM_LIMIT = 60 * 1024 * 1024
F32 = jnp.float32


def shape(*dims):
    return jax.ShapeDtypeStruct(dims, F32)


def halo_plan(ins, outs):
    field, cols = ins
    rows_in, cols_in = outs
    rows = field.shape[0]
    main, low, high = pl.ds(8, rows), pl.ds(0, 8), pl.ds(rows + 8, 8)
    first, last = pl.ds(0, 8), pl.ds(rows - 8, 8)
    one, two = pl.ds(0, 1), pl.ds(1, 2)
    remote = [
        (cols.at[one], cols_in.at[one, main], 0, 1),
        (cols.at[two], cols_in.at[two, main], 0, -1),
        (field.at[pl.ds(rows - 1, 1)], rows_in.at[one], 1, 0),
        (field.at[pl.ds(0, 2)], rows_in.at[two], -1, 0),
        (cols.at[one, last], cols_in.at[one, low], 1, 1),
        (cols.at[one, first], cols_in.at[one, high], -1, 1),
        (cols.at[two, last], cols_in.at[two, low], 1, -1),
        (cols.at[two, first], cols_in.at[two, high], -1, -1),
    ]
    return remote


def fold_plan(ins, outs):
    rows_out, cols = ins
    rows_in, cols_in = outs
    rows = cols.shape[1] - 16
    main, low, high = pl.ds(8, rows), pl.ds(0, 8), pl.ds(rows + 8, 8)
    one, two = pl.ds(0, 1), pl.ds(1, 2)
    remote = [
        (cols.at[one, main], cols_in.at[one, main], 0, -1),
        (cols.at[two, main], cols_in.at[two, main], 0, 1),
        (rows_out.at[one], rows_in.at[one], -1, 0),
        (rows_out.at[two], rows_in.at[two], 1, 0),
        (cols.at[one, low], cols_in.at[one, high], -1, -1),
        (cols.at[one, high], cols_in.at[one, low], 1, -1),
        (cols.at[two, low], cols_in.at[two, high], -1, 1),
        (cols.at[two, high], cols_in.at[two, low], 1, 1),
    ]
    return remote


def cubic_weights(f):
    return (
        -f * (f - 1.0) * (f - 2.0) * (1.0 / 6.0),
        (f + 1.0) * (f - 1.0) * (f - 2.0) * 0.5,
        -(f + 1.0) * f * (f - 2.0) * 0.5,
        (f + 1.0) * f * (f - 1.0) * (1.0 / 6.0),
    )


def code_weights(u, v, q):
    depth_shift = lax.shift_right_logical(q, 3)
    fractions = [u, v, jnp.bitwise_and(q, QF - 1)]
    return depth_shift, [cubic_weights(f.astype(F32) * (1.0 / QF)) for f in fractions]


def weighted(weights, terms):
    total = weights[0] * terms[0]
    for weight, term in zip(weights[1:], terms[1:]):
        total = total + weight * term
    return total


def pull_sides(window, weights):
    count = window.shape[0] - 3
    rows = weighted(weights[0], [window[r : r + count] for r in range(4)])
    return weighted(
        weights[1],
        [(rows if t == 0 else pltpu.roll(rows, LANES - t, 1))[:, :BY] for t in range(4)],
    )


def pull_depth(values, shift, weights):
    depth = values.shape[2]
    base = pltpu.roll(values, lax.rem(depth + 1 - shift, depth), 2)
    return weighted(
        weights[2], [base if m == 0 else pltpu.roll(base, depth - m, 2) for m in range(4)]
    )


def push_depth(values, shift, weights):
    depth = values.shape[2]
    base = pltpu.roll(values, lax.rem(depth - 1 + shift, depth), 2)
    return weighted(weights[2], [base if m == 0 else pltpu.roll(base, m, 2) for m in range(4)])


def correlated(w):
    taps = []
    for lag in range(4):
        tap = w[0] * w[lag]
        for m in range(1, 4 - lag):
            tap = tap + w[m] * w[m + lag]
        taps.append(tap)
    return taps


def push_sides(window, values_of, weights):
    carry = None
    for first in range(0, BX, CHUNK):
        values = values_of(first)
        depth = values.shape[2]
        wide = jnp.concatenate([values, jnp.zeros((CHUNK, LANES - BY, depth), F32)], axis=1)
        cols = weighted(weights[1], [wide if t == 0 else pltpu.roll(wide, t, 1) for t in range(4)])
        rows = []
        for i in range(CHUNK + 3):
            terms = [cols[i - r] * weights[0][r] for r in range(4) if 0 <= i - r < CHUNK]
            if carry is not None and i < 3:
                terms.append(carry[i])
            rows.append(sum(terms[1:], terms[0]))
        for i in range(CHUNK):
            window[first + i] = rows[i]
        carry = rows[CHUNK:]
    for i in range(3):
        window[BX + i] = carry[i]


def assemble(extended, field, rows_in, cols_in):
    rows = field.shape[0]
    extended[1 : rows + 1, 1 : BY + 1, :] = field[...]
    extended[0:1, 1 : BY + 1, :] = rows_in[0:1]
    extended[rows + 1 : rows + 3, 1 : BY + 1, :] = rows_in[1:3]
    for col, side in ((0, 0), (BY + 1, 1), (BY + 2, 2)):
        extended[:, col, :] = cols_in[side, 7 : rows + 10, :]


def emit_margins(total, acc, rows_out, cols_out):
    rows = total.shape[0]
    total[...] = acc[1 : rows + 1, 1 : BY + 1, :]
    rows_out[0:1] = acc[0:1, 1 : BY + 1, :]
    rows_out[1:3] = acc[rows + 1 : rows + 3, 1 : BY + 1, :]
    cols_out[...] = jnp.zeros_like(cols_out)
    for col, side in ((0, 0), (BY + 1, 1), (BY + 2, 2)):
        cols_out[side, 7 : rows + 10, :] = acc[:, col, :]


def gradient(states, rows_in, cols_in, step, block, blocks):
    rows, depth = states.shape[1], states.shape[3]
    first = block * BX
    cells = states[step, pl.ds(first, BX)]
    before = states[step, pl.ds(jnp.maximum(first - 1, 0), 1)]
    after = states[step, pl.ds(jnp.minimum(first + BX, rows - 1), 1)]
    before = jnp.where(block == 0, rows_in[0, pl.ds(step, 1)], before)
    after = jnp.where(block == blocks - 1, rows_in[1, pl.ds(step, 1)], after)
    left = cols_in[0, step, pl.ds(first, BX)][:, None, :]
    right = cols_in[1, step, pl.ds(first, BX)][:, None, :]
    col = lax.broadcasted_iota(jnp.int32, cells.shape, 1)
    below = jnp.concatenate([before, cells[:-1]], axis=0)
    above = jnp.concatenate([cells[1:], after], axis=0)
    lower = jnp.where(col == 0, left, pltpu.roll(cells, 1, 1))
    upper = jnp.where(col == BY - 1, right, pltpu.roll(cells, BY - 1, 1))
    return (
        (above - below) * 0.5,
        (upper - lower) * 0.5,
        (pltpu.roll(cells, depth - 1, 2) - pltpu.roll(cells, 1, 2)) * 0.5,
    )


def adjoints_kernel(
    n_gx, n_gy, pulls, owners, codes, states, velocity,
    force,
    states_v, velocity_v, rows_v, cols_v, edge_cols, request, requested_v, requested_s,
    field, edges, halo_rows, halo_cols, extended, supplied, later_v, inbox,
    next_field, next_edges, next_rows, next_cols, pushed, sums, acc,
    total, late_margin_rows, late_margin_cols, late_fold_rows, late_fold_cols, late,
    outbox, returned, early_margin_rows, early_margin_cols, early_fold_rows, early_fold_cols,
    early_slopes, brick, taps_high, taps_low, kept, rank, order, sorted_owner, save_sem, load_sem, send_sem, recv_sem, code_send, code_recv,
    brick_send, brick_recv, margin_send, margin_recv,
):
    gx, gy = lax.axis_index("gx"), lax.axis_index("gy")
    rows, depth = states.shape[1], states.shape[3]
    blocks, slots = rows // BX, n_gy * CAP

    def pull_of(k):
        return pulls[k]

    def owner_of(slot):
        return owners[0, 0, jnp.bitwise_and(slot, 1), lax.shift_right_logical(slot, 1)]

    def code_of(c, k):
        return codes[c, 0, k]

    def device(step_x, step_y):
        return (lax.rem(gx + step_x + n_gx, n_gx), lax.rem(gy + step_y + n_gy, n_gy))

    def remote(src, dst, send, recv, step_x, step_y):
        return pltpu.make_async_remote_copy(
            src_ref=src, dst_ref=dst, send_sem=send, recv_sem=recv,
            device_id=device(step_x, step_y), device_id_type=pl.DeviceIdType.MESH,
        )

    peers = [(i, j) for i in (-1, 1) for j in (-1, 0, 1)] + [(0, d) for d in range(1, n_gy)]
    barrier = pltpu.get_barrier_semaphore()
    for peer in peers:
        pl.semaphore_signal(
            barrier, inc=1, device_id=device(*peer), device_id_type=pl.DeviceIdType.MESH
        )
    loads = [
        pltpu.make_async_copy(states, states_v, load_sem.at[0]),
        pltpu.make_async_copy(velocity, velocity_v, load_sem.at[1]),
    ]
    for load in loads:
        load.start()
    peer_row = lax.broadcasted_iota(jnp.int32, request.shape, 0)
    entry = lax.broadcasted_iota(jnp.int32, request.shape, 1)
    lane = lax.broadcasted_iota(jnp.int32, request.shape, 2)
    place = jnp.where(entry < CAP, peer_row * CAP + entry, -1)
    table = jnp.zeros(request.shape, jnp.int32)
    for k in range(blocks):
        triple = jnp.where(
            lane == 0, code_of(0, k), jnp.where(lane == 1, code_of(1, k), code_of(2, k))
        )
        table = jnp.where(place == pull_of(k), triple, table)
    request[...] = table
    requested_v[pl.ds(gy, 1)] = request[pl.ds(gy, 1)]
    loads[0].wait()
    for step in range(STEPS):
        edge_cols[0, step] = states_v[step, :, BY - 1, :]
        edge_cols[1, step] = states_v[step, :, 0, :]
    pl.semaphore_wait(barrier, len(peers))

    copies = [
        remote(edge_cols.at[0], cols_v.at[0], send_sem.at[0], recv_sem.at[0], 0, 1),
        remote(edge_cols.at[1], cols_v.at[1], send_sem.at[1], recv_sem.at[1], 0, -1),
        remote(states_v.at[:, rows - 1], rows_v.at[0], send_sem.at[2], recv_sem.at[2], 1, 0),
        remote(states_v.at[:, 0], rows_v.at[1], send_sem.at[3], recv_sem.at[3], -1, 0),
    ]
    for copy in copies:
        copy.start()
    code_copies = []
    for d in range(1, n_gy):
        peer = lax.rem(gy + d, n_gy)
        code_copies.append(
            remote(request.at[peer], requested_v.at[gy], code_send.at[d], code_recv.at[d], 0, d)
        )
    for copy in code_copies:
        copy.start()
    loads[1].wait()
    for copy in copies:
        copy.wait()

    @pl.loop(0, blocks)
    def _(block):
        cells = pl.ds(block * BX, BX)
        terms = []
        for step in range(STEPS):
            parts = gradient(states_v, rows_v, cols_v, step, block, blocks)
            terms.append(
                (
                    velocity_v[0, cells] * parts[0]
                    + velocity_v[1, cells] * parts[1]
                    + velocity_v[2, cells] * parts[2]
                )
                * -STEP_SIZE
            )
        field[cells] = terms[0]
        for side, col in ((0, BY - 1), (1, 0), (2, 1)):
            edges[side, cells] = terms[0][:, col, :]
        later_v[cells] = terms[1]

    def margin_copies(phase, moves):
        copies = [
            remote(src, dst, margin_send.at[phase, i], margin_recv.at[phase, i], step_x, step_y)
            for i, (src, dst, step_x, step_y) in enumerate(moves)
        ]
        for copy in copies:
            copy.start()
        return copies

    copies = margin_copies(0, halo_plan((field, edges), (halo_rows, halo_cols)))
    for copy in code_copies:
        copy.wait()
    table_copy = pltpu.make_async_copy(requested_v, requested_s, load_sem.at[2])
    table_copy.start()
    table_copy.wait()
    for copy in copies:
        copy.wait()
    assemble(extended, field, halo_rows, halo_cols)

    def codes_of(slot):
        peer, e = lax.shift_right_logical(slot, 1), jnp.bitwise_and(slot, 1)
        return code_weights(*[requested_s[peer, e, c] for c in range(3)])

    def supply(peer, target):
        for e in range(CAP):
            slot = peer * CAP + e
            first = jnp.maximum(owner_of(slot), 0) * BX
            shift, weights = codes_of(slot)
            for row in range(0, BX, CHUNK):
                sides = pull_sides(extended[pl.ds(first + row, CHUNK + 3)], weights)
                target[slot, row : row + CHUNK] = pull_depth(sides, shift, weights)

    def brick_copy(phase, d, source, target):
        peer = lax.rem(gy + d, n_gy)
        return remote(
            source.at[pl.ds(peer * CAP, CAP)], target.at[pl.ds(gy * CAP, CAP)],
            brick_send.at[phase, d], brick_recv.at[phase, d], 0, d,
        )

    @pl.loop(1, n_gy)
    def _(d):
        supply(lax.rem(gy + d, n_gy), supplied)
        brick_copy(0, d, supplied, inbox).start()

    supply(gy, inbox)

    @pl.loop(0, slots)
    def _(s):
        _, weights = codes_of(s)
        for axis in range(3):
            for m in range(4):
                kept[s, 4 * axis + m] = weights[axis][m]
        taps = correlated(weights[2])
        row = lax.broadcasted_iota(jnp.int32, (depth, depth), 0)
        col = lax.broadcasted_iota(jnp.int32, (depth, depth), 1)
        gap = jnp.abs(row - col)
        gap = jnp.minimum(gap, depth - gap)
        matrix = jnp.zeros((depth, depth), F32)
        for lag in range(4):
            matrix = jnp.where(gap == lag, taps[lag], matrix)
        high = matrix.astype(jnp.bfloat16)
        taps_high[s] = high
        taps_low[s] = (matrix - high.astype(F32)).astype(jnp.bfloat16)

    def kept_weights(slot):
        return [[kept[slot, 4 * axis + m] for m in range(4)] for axis in range(3)]

    def correlate(slot, values):
        high = values.astype(jnp.bfloat16)
        low = (values - high.astype(F32)).astype(jnp.bfloat16)

        def dot(left, right):
            return jnp.dot(left, right, preferred_element_type=F32)

        return (
            dot(high, taps_low[slot]) + dot(low, taps_high[slot]) + dot(high, taps_high[slot])
        )

    @pl.loop(0, slots)
    def _(s):
        mine = owner_of(s)

        def ahead(t, count):
            other = owner_of(t)
            before = jnp.logical_or(other < mine, jnp.logical_and(other == mine, t < s))
            return count + jnp.where(before, 1, 0)

        rank[s] = lax.fori_loop(0, slots, ahead, 0)

    @pl.loop(0, slots)
    def _(j):
        found = lax.fori_loop(0, slots, lambda t, at: jnp.where(rank[t] == j, t, at), 0)
        order[j] = found
        sorted_owner[j] = owner_of(found)

    @pl.loop(1, n_gy)
    def _(d):
        brick_copy(0, d, supplied, inbox).wait()

    @pl.loop(0, blocks)
    def _(block):
        cells = pl.ds(block * BX, BX)
        values = inbox[pull_of(block)] + later_v[cells]
        next_field[cells] = values
        for side, col in ((0, BY - 1), (1, 0), (2, 1)):
            next_edges[side, cells] = values[:, col, :]

    for copy in margin_copies(1, halo_plan((next_field, next_edges), (next_rows, next_cols))):
        copy.wait()
    assemble(extended, next_field, next_rows, next_cols)

    def accumulate():
        sums[0] = jnp.zeros(sums.shape[1:], F32)

        @pl.loop(0, slots)
        def _(j):
            before = jnp.maximum(j - 1, 0)
            same = sorted_owner[j] == sorted_owner[before]
            sums[j] = jnp.where(same, sums[before], 0.0) + pushed[order[j]]

        acc[...] = jnp.zeros_like(acc)

        @pl.loop(0, blocks)
        def _(k):
            def at_most(t, count):
                return count + jnp.where(sorted_owner[t] <= k, 1, 0)

            last = jnp.maximum(lax.fori_loop(0, slots, at_most, 0) - 1, 0)
            window = pl.ds(k * BX, WIN)
            acc[window] = acc[window] + jnp.where(sorted_owner[last] == k, sums[last], 0.0)

    def fold_all(fold_rows, fold_cols, target):
        @pl.loop(0, blocks)
        def _(block):
            cells = pl.ds(block * BX, BX)
            target[cells] = fold(total[cells], fold_rows, fold_cols, block, blocks)

    @pl.loop(0, slots)
    def _(slot):
        first = jnp.maximum(owner_of(slot), 0) * BX
        weights = kept_weights(slot)
        for row in range(0, BX, CHUNK):
            brick[row : row + CHUNK] = pull_sides(
                extended[pl.ds(first + row, CHUNK + 3)], weights
            )
        values = correlate(slot, brick[...].reshape(BX * BY, depth))
        brick[...] = values.reshape(BX, BY, depth)
        push_sides(pushed.at[slot], lambda row: brick[row : row + CHUNK], weights)

    accumulate()
    emit_margins(total, acc, late_margin_rows, late_margin_cols)
    moves = fold_plan((late_margin_rows, late_margin_cols), (late_fold_rows, late_fold_cols))
    for copy in margin_copies(2, moves):
        copy.wait()
    fold_all(late_fold_rows, late_fold_cols, late)
    def fill(peer, target):
        for e in range(CAP):
            slot = peer * CAP + e
            source = 0
            for k in range(1, blocks):
                source = jnp.where(pull_of(k) == slot, k, source)
            target[slot] = late[pl.ds(source * BX, BX)]

    @pl.loop(1, n_gy)
    def _(d):
        fill(lax.rem(gy + d, n_gy), outbox)
        brick_copy(1, d, outbox, returned).start()

    fill(gy, returned)

    @pl.loop(0, blocks)
    def _(block):
        cells = pl.ds(block * BX, BX)
        scaled = late[cells] * -STEP_SIZE
        parts = gradient(states_v, rows_v, cols_v, 1, block, blocks)
        slopes = gradient(states_v, rows_v, cols_v, 0, block, blocks)
        for c in range(3):
            velocity_v[c, cells] = scaled * parts[c]
            early_slopes[c, cells] = slopes[c]

    def push(peer):
        for e in range(CAP):
            slot = peer * CAP + e
            peer_row, e_row = lax.shift_right_logical(slot, 1), jnp.bitwise_and(slot, 1)
            shift = lax.shift_right_logical(requested_s[peer_row, e_row, 2], 3)
            weights = kept_weights(slot)
            push_sides(
                pushed.at[slot],
                lambda row: push_depth(returned[slot, row : row + CHUNK], shift, weights),
                weights,
            )

    push(gy)

    @pl.loop(1, n_gy)
    def _(d):
        brick_copy(1, d, outbox, returned).wait()
        push(lax.rem(gy + n_gy - d, n_gy))

    accumulate()
    emit_margins(total, acc, early_margin_rows, early_margin_cols)
    moves = fold_plan((early_margin_rows, early_margin_cols), (early_fold_rows, early_fold_cols))
    for copy in margin_copies(3, moves):
        copy.wait()

    def save(block):
        cells = pl.ds(block * BX, BX)
        return pltpu.make_async_copy(
            velocity_v.at[:, cells], force.at[:, cells], save_sem.at[block]
        )

    @pl.loop(0, blocks)
    def _(block):
        cells = pl.ds(block * BX, BX)
        early = fold(total[cells], early_fold_rows, early_fold_cols, block, blocks)
        scaled = early * -STEP_SIZE
        for c in range(3):
            velocity_v[c, cells] = velocity_v[c, cells] + scaled * early_slopes[c, cells]
        save(block).start()

    @pl.loop(0, blocks)
    def _(block):
        save(block).wait()


def adjoints_call(states, velocity, pulls, owners, codes):
    n_gx, n_gy = lax.axis_size("gx"), lax.axis_size("gy")
    _, rows, cols, depth = states.shape
    slots = n_gy * CAP
    table = (n_gy, 8, 128)
    hbm = pl.BlockSpec(memory_space=pltpu.HBM)
    dma = pltpu.SemaphoreType.DMA

    def vmem(*dims):
        return pltpu.VMEM(dims, F32)

    field = vmem(rows, cols, depth)
    edges = vmem(3, rows, depth)
    margin_rows, margin_cols = vmem(3, cols, depth), vmem(3, rows + 16, depth)
    extended = vmem(rows + 3, LANES, depth)
    bricks = vmem(slots, BX, BY, depth)
    margins = [margin_rows, margin_cols]
    return pl.pallas_call(
        lambda *refs: adjoints_kernel(n_gx, n_gy, *refs),
        name="adjoints",
        in_specs=[pl.BlockSpec(memory_space=pltpu.SMEM)] * 3 + [hbm, hbm],
        out_specs=hbm,
        out_shape=shape(3, rows, cols, depth),
        scratch_shapes=[
            vmem(STEPS, rows, cols, depth),
            vmem(3, rows, cols, depth),
            vmem(2, STEPS, cols, depth),
            vmem(2, STEPS, rows, depth),
            vmem(2, STEPS, rows, depth),
            pltpu.VMEM(table, jnp.int32),
            pltpu.VMEM(table, jnp.int32),
            pltpu.SMEM(table, jnp.int32),
            field,
            edges,
            *margins,
            extended,
            bricks,
            field,
            bricks,
            field,
            edges,
            *margins,
            vmem(slots, WIN, LANES, depth),
            vmem(slots, WIN, LANES, depth),
            extended,
            field,
            *margins,
            *margins,
            field,
            bricks,
            bricks,
            *margins,
            *margins,
            vmem(3, rows, cols, depth),
            vmem(BX, BY, depth),
            pltpu.VMEM((slots, depth, depth), jnp.bfloat16),
            pltpu.VMEM((slots, depth, depth), jnp.bfloat16),
            pltpu.SMEM((slots, 12), F32),
            pltpu.SMEM((slots,), jnp.int32),
            pltpu.SMEM((slots,), jnp.int32),
            pltpu.SMEM((slots,), jnp.int32),
            dma((rows // BX,)),
            dma((3,)),
            dma((4,)),
            dma((4,)),
            dma((n_gy,)),
            dma((n_gy,)),
            dma((2, n_gy)),
            dma((2, n_gy)),
            dma((4, 8)),
            dma((4, 8)),
        ],
        compiler_params=pltpu.CompilerParams(
            collective_id=0, has_side_effects=True, vmem_limit_bytes=VMEM_LIMIT
        ),
    )(pulls, owners, codes, states, velocity)


def fold(values, rows_in, cols_in, block, blocks):
    depth = values.shape[2]
    is_first, is_last = block == 0, block == blocks - 1
    rows = cols_in.shape[1] - 16
    zeros = jnp.zeros((8, depth), F32)
    col = lax.broadcasted_iota(jnp.int32, values.shape, 1)
    row = lax.broadcasted_iota(jnp.int32, values.shape, 0)
    values = values + jnp.where(jnp.logical_and(is_last, row == BX - 1), rows_in[0:1], 0.0)
    for i in range(2):
        values = values + jnp.where(
            jnp.logical_and(is_first, row == i), rows_in[1 + i : 2 + i], 0.0
        )
    for side, place in ((0, BY - 1), (1, 0), (2, 1)):
        strip = cols_in[side, pl.ds(8 + block * BX, BX)]
        low = jnp.concatenate([cols_in[side, 0:8], zeros], axis=0)
        high = jnp.concatenate([zeros, cols_in[side, rows + 8 : rows + 16]], axis=0)
        strip = strip + jnp.where(is_first, low, 0.0) + jnp.where(is_last, high, 0.0)
        values = values + jnp.where(col == place, strip[:, None, :], 0.0)
    return values


def body(velocity, states, pull_plan, send_plan, codes):
    _, rows, cols, depth = velocity.shape
    assert cols == BY and rows % BX == 0
    return adjoints_call(
        states,
        velocity,
        pull_plan.reshape(rows // BX),
        send_plan.transpose(0, 1, 3, 2),
        codes.transpose(0, 2, 1),
    )


def solution(mesh):
    return jax.shard_map(
        body,
        mesh=mesh,
        in_specs=(
            P(None, "gx", "gy", None),
            P(None, "gx", "gy", None),
            P("gx", "gy"),
            P("gx", "gy", None, None),
            P(None, "gx", "gy"),
        ),
        out_specs=P(None, "gx", "gy", None),
        check_vma=False,
    )
```

```python
import functools

import jax
import jax.numpy as jnp
from jax import lax
from jax.experimental import pallas as pl
from jax.experimental.pallas import tpu as pltpu
from jax.sharding import PartitionSpec as P

BX = 16
BY = 16
CAP = 2
QF = 8
STEPS = 2
STEP_SIZE = 1.0 / STEPS
WIN = BX + 3
CHUNK = 4
LANES = 24
VMEM_LIMIT = 60 * 1024 * 1024
F32 = jnp.float32


def shape(*dims):
    return jax.ShapeDtypeStruct(dims, F32)


def halo_plan(ins, outs):
    field, cols = ins
    rows_in, cols_in = outs
    rows = field.shape[0]
    main, low, high = pl.ds(8, rows), pl.ds(0, 8), pl.ds(rows + 8, 8)
    first, last = pl.ds(0, 8), pl.ds(rows - 8, 8)
    one, two = pl.ds(0, 1), pl.ds(1, 2)
    remote = [
        (cols.at[one], cols_in.at[one, main], 0, 1),
        (cols.at[two], cols_in.at[two, main], 0, -1),
        (field.at[pl.ds(rows - 1, 1)], rows_in.at[one], 1, 0),
        (field.at[pl.ds(0, 2)], rows_in.at[two], -1, 0),
        (cols.at[one, last], cols_in.at[one, low], 1, 1),
        (cols.at[one, first], cols_in.at[one, high], -1, 1),
        (cols.at[two, last], cols_in.at[two, low], 1, -1),
        (cols.at[two, first], cols_in.at[two, high], -1, -1),
    ]
    return remote


def fold_plan(ins, outs):
    rows_out, cols = ins
    rows_in, cols_in = outs
    rows = cols.shape[1] - 16
    main, low, high = pl.ds(8, rows), pl.ds(0, 8), pl.ds(rows + 8, 8)
    one, two = pl.ds(0, 1), pl.ds(1, 2)
    remote = [
        (cols.at[one, main], cols_in.at[one, main], 0, -1),
        (cols.at[two, main], cols_in.at[two, main], 0, 1),
        (rows_out.at[one], rows_in.at[one], -1, 0),
        (rows_out.at[two], rows_in.at[two], 1, 0),
        (cols.at[one, low], cols_in.at[one, high], -1, -1),
        (cols.at[one, high], cols_in.at[one, low], 1, -1),
        (cols.at[two, low], cols_in.at[two, high], -1, 1),
        (cols.at[two, high], cols_in.at[two, low], 1, 1),
    ]
    return remote


def cubic_weights(f):
    return (
        -f * (f - 1.0) * (f - 2.0) * (1.0 / 6.0),
        (f + 1.0) * (f - 1.0) * (f - 2.0) * 0.5,
        -(f + 1.0) * f * (f - 2.0) * 0.5,
        (f + 1.0) * f * (f - 1.0) * (1.0 / 6.0),
    )


def code_weights(u, v, q):
    depth_shift = lax.shift_right_logical(q, 3)
    fractions = [u, v, jnp.bitwise_and(q, QF - 1)]
    return depth_shift, [cubic_weights(f.astype(F32) * (1.0 / QF)) for f in fractions]


def weighted(weights, terms):
    total = weights[0] * terms[0]
    for weight, term in zip(weights[1:], terms[1:]):
        total = total + weight * term
    return total


def pull_sides(window, weights):
    count = window.shape[0] - 3
    rows = weighted(weights[0], [window[r : r + count] for r in range(4)])
    return weighted(
        weights[1],
        [(rows if t == 0 else pltpu.roll(rows, LANES - t, 1))[:, :BY] for t in range(4)],
    )


def pull_depth(values, shift, weights):
    depth = values.shape[2]
    base = pltpu.roll(values, lax.rem(depth + 1 - shift, depth), 2)
    return weighted(
        weights[2], [base if m == 0 else pltpu.roll(base, depth - m, 2) for m in range(4)]
    )


def push_depth(values, shift, weights):
    depth = values.shape[2]
    base = pltpu.roll(values, lax.rem(depth - 1 + shift, depth), 2)
    return weighted(weights[2], [base if m == 0 else pltpu.roll(base, m, 2) for m in range(4)])


def correlated(w):
    taps = []
    for lag in range(4):
        tap = w[0] * w[lag]
        for m in range(1, 4 - lag):
            tap = tap + w[m] * w[m + lag]
        taps.append(tap)
    return taps


def push_sides(window, values_of, weights):
    carry = None
    for first in range(0, BX, CHUNK):
        values = values_of(first)
        depth = values.shape[2]
        wide = jnp.concatenate([values, jnp.zeros((CHUNK, LANES - BY, depth), F32)], axis=1)
        cols = weighted(weights[1], [wide if t == 0 else pltpu.roll(wide, t, 1) for t in range(4)])
        rows = []
        for i in range(CHUNK + 3):
            terms = [cols[i - r] * weights[0][r] for r in range(4) if 0 <= i - r < CHUNK]
            if carry is not None and i < 3:
                terms.append(carry[i])
            rows.append(sum(terms[1:], terms[0]))
        for i in range(CHUNK):
            window[first + i] = rows[i]
        carry = rows[CHUNK:]
    for i in range(3):
        window[BX + i] = carry[i]


def assemble(extended, field, rows_in, cols_in):
    rows = field.shape[0]
    extended[1 : rows + 1, 1 : BY + 1, :] = field[...]
    extended[0:1, 1 : BY + 1, :] = rows_in[0:1]
    extended[rows + 1 : rows + 3, 1 : BY + 1, :] = rows_in[1:3]
    for col, side in ((0, 0), (BY + 1, 1), (BY + 2, 2)):
        extended[:, col, :] = cols_in[side, 7 : rows + 10, :]


def emit_margins(total, acc, rows_out, cols_out):
    rows = total.shape[0]
    total[...] = acc[1 : rows + 1, 1 : BY + 1, :]
    rows_out[0:1] = acc[0:1, 1 : BY + 1, :]
    rows_out[1:3] = acc[rows + 1 : rows + 3, 1 : BY + 1, :]
    cols_out[...] = jnp.zeros_like(cols_out)
    for col, side in ((0, 0), (BY + 1, 1), (BY + 2, 2)):
        cols_out[side, 7 : rows + 10, :] = acc[:, col, :]


def gradient(states, rows_in, cols_in, step, block, blocks):
    rows, depth = states.shape[1], states.shape[3]
    first = block * BX
    cells = states[step, pl.ds(first, BX)]
    before = states[step, pl.ds(jnp.maximum(first - 1, 0), 1)]
    after = states[step, pl.ds(jnp.minimum(first + BX, rows - 1), 1)]
    before = jnp.where(block == 0, rows_in[0, pl.ds(step, 1)], before)
    after = jnp.where(block == blocks - 1, rows_in[1, pl.ds(step, 1)], after)
    left = cols_in[0, step, pl.ds(first, BX)][:, None, :]
    right = cols_in[1, step, pl.ds(first, BX)][:, None, :]
    col = lax.broadcasted_iota(jnp.int32, cells.shape, 1)
    below = jnp.concatenate([before, cells[:-1]], axis=0)
    above = jnp.concatenate([cells[1:], after], axis=0)
    lower = jnp.where(col == 0, left, pltpu.roll(cells, 1, 1))
    upper = jnp.where(col == BY - 1, right, pltpu.roll(cells, BY - 1, 1))
    return (
        (above - below) * 0.5,
        (upper - lower) * 0.5,
        (pltpu.roll(cells, depth - 1, 2) - pltpu.roll(cells, 1, 2)) * 0.5,
    )


def adjoints_kernel(
    n_gx, n_gy, pulls, owners, codes, states, velocity,
    force,
    states_v, velocity_v, rows_v, cols_v, edge_cols, request, requested_v, requested_s,
    field, edges, halo_rows, halo_cols, extended, supplied, later_v, inbox,
    next_field, next_edges, next_rows, next_cols, pushed, sums, acc,
    total, late_margin_rows, late_margin_cols, late_fold_rows, late_fold_cols, late,
    outbox, returned, early_margin_rows, early_margin_cols, early_fold_rows, early_fold_cols,
    early_slopes, brick, taps_high, taps_low, kept, rank, order, sorted_owner, save_sem, load_sem, send_sem, recv_sem, code_send, code_recv,
    brick_send, brick_recv, margin_send, margin_recv,
):
    gx, gy = lax.axis_index("gx"), lax.axis_index("gy")
    rows, depth = states.shape[1], states.shape[3]
    blocks, slots = rows // BX, n_gy * CAP

    def pull_of(k):
        return pulls[k]

    def owner_of(slot):
        return owners[0, 0, jnp.bitwise_and(slot, 1), lax.shift_right_logical(slot, 1)]

    def code_of(c, k):
        return codes[c, 0, k]

    def device(step_x, step_y):
        return (lax.rem(gx + step_x + n_gx, n_gx), lax.rem(gy + step_y + n_gy, n_gy))

    def remote(src, dst, send, recv, step_x, step_y):
        return pltpu.make_async_remote_copy(
            src_ref=src, dst_ref=dst, send_sem=send, recv_sem=recv,
            device_id=device(step_x, step_y), device_id_type=pl.DeviceIdType.MESH,
        )

    peers = [(i, j) for i in (-1, 1) for j in (-1, 0, 1)] + [(0, d) for d in range(1, n_gy)]
    barrier = pltpu.get_barrier_semaphore()
    for peer in peers:
        pl.semaphore_signal(
            barrier, inc=1, device_id=device(*peer), device_id_type=pl.DeviceIdType.MESH
        )
    loads = [
        pltpu.make_async_copy(states, states_v, load_sem.at[0]),
        pltpu.make_async_copy(velocity, velocity_v, load_sem.at[1]),
    ]
    for load in loads:
        load.start()
    peer_row = lax.broadcasted_iota(jnp.int32, request.shape, 0)
    entry = lax.broadcasted_iota(jnp.int32, request.shape, 1)
    lane = lax.broadcasted_iota(jnp.int32, request.shape, 2)
    place = jnp.where(entry < CAP, peer_row * CAP + entry, -1)
    table = jnp.zeros(request.shape, jnp.int32)
    for k in range(blocks):
        triple = jnp.where(
            lane == 0, code_of(0, k), jnp.where(lane == 1, code_of(1, k), code_of(2, k))
        )
        table = jnp.where(place == pull_of(k), triple, table)
    request[...] = table
    requested_v[pl.ds(gy, 1)] = request[pl.ds(gy, 1)]
    loads[0].wait()
    for step in range(STEPS):
        edge_cols[0, step] = states_v[step, :, BY - 1, :]
        edge_cols[1, step] = states_v[step, :, 0, :]
    pl.semaphore_wait(barrier, len(peers))

    copies = [
        remote(edge_cols.at[0], cols_v.at[0], send_sem.at[0], recv_sem.at[0], 0, 1),
        remote(edge_cols.at[1], cols_v.at[1], send_sem.at[1], recv_sem.at[1], 0, -1),
        remote(states_v.at[:, rows - 1], rows_v.at[0], send_sem.at[2], recv_sem.at[2], 1, 0),
        remote(states_v.at[:, 0], rows_v.at[1], send_sem.at[3], recv_sem.at[3], -1, 0),
    ]
    for copy in copies:
        copy.start()
    code_copies = []
    for d in range(1, n_gy):
        peer = lax.rem(gy + d, n_gy)
        code_copies.append(
            remote(request.at[peer], requested_v.at[gy], code_send.at[d], code_recv.at[d], 0, d)
        )
    for copy in code_copies:
        copy.start()
    loads[1].wait()
    for copy in copies:
        copy.wait()

    @pl.loop(0, blocks)
    def _(block):
        cells = pl.ds(block * BX, BX)
        terms = []
        for step in range(STEPS):
            parts = gradient(states_v, rows_v, cols_v, step, block, blocks)
            terms.append(
                (
                    velocity_v[0, cells] * parts[0]
                    + velocity_v[1, cells] * parts[1]
                    + velocity_v[2, cells] * parts[2]
                )
                * -STEP_SIZE
            )
        field[cells] = terms[0]
        for side, col in ((0, BY - 1), (1, 0), (2, 1)):
            edges[side, cells] = terms[0][:, col, :]
        later_v[cells] = terms[1]

    def margin_copies(phase, moves):
        copies = [
            remote(src, dst, margin_send.at[phase, i], margin_recv.at[phase, i], step_x, step_y)
            for i, (src, dst, step_x, step_y) in enumerate(moves)
        ]
        for copy in copies:
            copy.start()
        return copies

    copies = margin_copies(0, halo_plan((field, edges), (halo_rows, halo_cols)))
    for copy in code_copies:
        copy.wait()
    table_copy = pltpu.make_async_copy(requested_v, requested_s, load_sem.at[2])
    table_copy.start()
    table_copy.wait()
    for copy in copies:
        copy.wait()
    assemble(extended, field, halo_rows, halo_cols)

    def codes_of(slot):
        peer, e = lax.shift_right_logical(slot, 1), jnp.bitwise_and(slot, 1)
        return code_weights(*[requested_s[peer, e, c] for c in range(3)])

    def supply(peer, target):
        for e in range(CAP):
            slot = peer * CAP + e
            first = jnp.maximum(owner_of(slot), 0) * BX
            shift, weights = codes_of(slot)
            for row in range(0, BX, CHUNK):
                sides = pull_sides(extended[pl.ds(first + row, CHUNK + 3)], weights)
                target[slot, row : row + CHUNK] = pull_depth(sides, shift, weights)

    def brick_copy(phase, d, source, target):
        peer = lax.rem(gy + d, n_gy)
        return remote(
            source.at[pl.ds(peer * CAP, CAP)], target.at[pl.ds(gy * CAP, CAP)],
            brick_send.at[phase, d], brick_recv.at[phase, d], 0, d,
        )

    @pl.loop(1, n_gy)
    def _(d):
        supply(lax.rem(gy + d, n_gy), supplied)
        brick_copy(0, d, supplied, inbox).start()

    supply(gy, inbox)

    @pl.loop(0, slots)
    def _(s):
        _, weights = codes_of(s)
        for axis in range(3):
            for m in range(4):
                kept[s, 4 * axis + m] = weights[axis][m]
        taps = correlated(weights[2])
        row = lax.broadcasted_iota(jnp.int32, (depth, depth), 0)
        col = lax.broadcasted_iota(jnp.int32, (depth, depth), 1)
        gap = jnp.abs(row - col)
        gap = jnp.minimum(gap, depth - gap)
        matrix = jnp.zeros((depth, depth), F32)
        for lag in range(4):
            matrix = jnp.where(gap == lag, taps[lag], matrix)
        high = matrix.astype(jnp.bfloat16)
        taps_high[s] = high
        taps_low[s] = (matrix - high.astype(F32)).astype(jnp.bfloat16)

    def kept_weights(slot):
        return [[kept[slot, 4 * axis + m] for m in range(4)] for axis in range(3)]

    def correlate(slot, values):
        high = values.astype(jnp.bfloat16)
        low = (values - high.astype(F32)).astype(jnp.bfloat16)

        def dot(left, right):
            return jnp.dot(left, right, preferred_element_type=F32)

        return (
            dot(high, taps_low[slot]) + dot(low, taps_high[slot]) + dot(high, taps_high[slot])
        )

    @pl.loop(0, slots)
    def _(s):
        mine = owner_of(s)

        def ahead(t, count):
            other = owner_of(t)
            before = jnp.logical_or(other < mine, jnp.logical_and(other == mine, t < s))
            return count + jnp.where(before, 1, 0)

        rank[s] = lax.fori_loop(0, slots, ahead, 0)

    @pl.loop(0, slots)
    def _(j):
        found = lax.fori_loop(0, slots, lambda t, at: jnp.where(rank[t] == j, t, at), 0)
        order[j] = found
        sorted_owner[j] = owner_of(found)

    @pl.loop(1, n_gy)
    def _(d):
        brick_copy(0, d, supplied, inbox).wait()

    @pl.loop(0, blocks)
    def _(block):
        cells = pl.ds(block * BX, BX)
        values = inbox[pull_of(block)] + later_v[cells]
        next_field[cells] = values
        for side, col in ((0, BY - 1), (1, 0), (2, 1)):
            next_edges[side, cells] = values[:, col, :]

    for copy in margin_copies(1, halo_plan((next_field, next_edges), (next_rows, next_cols))):
        copy.wait()
    assemble(extended, next_field, next_rows, next_cols)

    def accumulate():
        sums[0] = jnp.zeros(sums.shape[1:], F32)

        @pl.loop(0, slots)
        def _(j):
            before = jnp.maximum(j - 1, 0)
            same = sorted_owner[j] == sorted_owner[before]
            sums[j] = jnp.where(same, sums[before], 0.0) + pushed[order[j]]

        acc[...] = jnp.zeros_like(acc)

        @pl.loop(0, blocks)
        def _(k):
            def at_most(t, count):
                return count + jnp.where(sorted_owner[t] <= k, 1, 0)

            last = jnp.maximum(lax.fori_loop(0, slots, at_most, 0) - 1, 0)
            window = pl.ds(k * BX, WIN)
            acc[window] = acc[window] + jnp.where(sorted_owner[last] == k, sums[last], 0.0)

    def fold_all(fold_rows, fold_cols, target):
        @pl.loop(0, blocks)
        def _(block):
            cells = pl.ds(block * BX, BX)
            target[cells] = fold(total[cells], fold_rows, fold_cols, block, blocks)

    @pl.loop(0, slots)
    def _(slot):
        first = jnp.maximum(owner_of(slot), 0) * BX
        weights = kept_weights(slot)
        for row in range(0, BX, CHUNK):
            brick[row : row + CHUNK] = pull_sides(
                extended[pl.ds(first + row, CHUNK + 3)], weights
            )
        values = correlate(slot, brick[...].reshape(BX * BY, depth))
        brick[...] = values.reshape(BX, BY, depth)
        push_sides(pushed.at[slot], lambda row: brick[row : row + CHUNK], weights)

    accumulate()
    emit_margins(total, acc, late_margin_rows, late_margin_cols)
    moves = fold_plan((late_margin_rows, late_margin_cols), (late_fold_rows, late_fold_cols))
    for copy in margin_copies(2, moves):
        copy.wait()
    fold_all(late_fold_rows, late_fold_cols, late)
    def fill(peer, target):
        for e in range(CAP):
            slot = peer * CAP + e
            source = 0
            for k in range(1, blocks):
                source = jnp.where(pull_of(k) == slot, k, source)
            target[slot] = late[pl.ds(source * BX, BX)]

    wave = n_gy // 2
    rest = n_gy - wave

    @pl.loop(1, n_gy)
    def _(d):
        fill(lax.rem(gy + d, n_gy), outbox)

    @pl.loop(1, wave + 1)
    def _(d):
        brick_copy(1, d, outbox, returned).start()

    fill(gy, returned)

    @pl.loop(0, blocks)
    def _(block):
        cells = pl.ds(block * BX, BX)
        scaled = late[cells] * -STEP_SIZE
        parts = gradient(states_v, rows_v, cols_v, 1, block, blocks)
        slopes = gradient(states_v, rows_v, cols_v, 0, block, blocks)
        for c in range(3):
            velocity_v[c, cells] = scaled * parts[c]
            early_slopes[c, cells] = slopes[c]

    def push(peer):
        for e in range(CAP):
            slot = peer * CAP + e
            peer_row, e_row = lax.shift_right_logical(slot, 1), jnp.bitwise_and(slot, 1)
            shift = lax.shift_right_logical(requested_s[peer_row, e_row, 2], 3)
            weights = kept_weights(slot)
            push_sides(
                pushed.at[slot],
                lambda row: push_depth(returned[slot, row : row + CHUNK], shift, weights),
                weights,
            )

    @pl.loop(1, rest)
    def _(d):
        brick_copy(1, d, outbox, returned).wait_send()
        brick_copy(1, d + wave, outbox, returned).start()

    push(gy)

    @pl.loop(1, rest)
    def _(d):
        brick_copy(1, d, outbox, returned).wait_recv()
        push(lax.rem(gy + n_gy - d, n_gy))

    @pl.loop(rest, n_gy)
    def _(d):
        brick_copy(1, d, outbox, returned).wait()
        push(lax.rem(gy + n_gy - d, n_gy))

    accumulate()
    emit_margins(total, acc, early_margin_rows, early_margin_cols)
    moves = fold_plan((early_margin_rows, early_margin_cols), (early_fold_rows, early_fold_cols))
    for copy in margin_copies(3, moves):
        copy.wait()

    def save(block):
        cells = pl.ds(block * BX, BX)
        return pltpu.make_async_copy(
            velocity_v.at[:, cells], force.at[:, cells], save_sem.at[block]
        )

    @pl.loop(0, blocks)
    def _(block):
        cells = pl.ds(block * BX, BX)
        early = fold(total[cells], early_fold_rows, early_fold_cols, block, blocks)
        scaled = early * -STEP_SIZE
        for c in range(3):
            velocity_v[c, cells] = velocity_v[c, cells] + scaled * early_slopes[c, cells]
        save(block).start()

    @pl.loop(0, blocks)
    def _(block):
        save(block).wait()


def adjoints_call(states, velocity, pulls, owners, codes):
    n_gx, n_gy = lax.axis_size("gx"), lax.axis_size("gy")
    _, rows, cols, depth = states.shape
    slots = n_gy * CAP
    table = (n_gy, 8, 128)
    hbm = pl.BlockSpec(memory_space=pltpu.HBM)
    dma = pltpu.SemaphoreType.DMA

    def vmem(*dims):
        return pltpu.VMEM(dims, F32)

    field = vmem(rows, cols, depth)
    edges = vmem(3, rows, depth)
    margin_rows, margin_cols = vmem(3, cols, depth), vmem(3, rows + 16, depth)
    extended = vmem(rows + 3, LANES, depth)
    bricks = vmem(slots, BX, BY, depth)
    margins = [margin_rows, margin_cols]
    return pl.pallas_call(
        lambda *refs: adjoints_kernel(n_gx, n_gy, *refs),
        name="adjoints",
        in_specs=[pl.BlockSpec(memory_space=pltpu.SMEM)] * 3 + [hbm, hbm],
        out_specs=hbm,
        out_shape=shape(3, rows, cols, depth),
        scratch_shapes=[
            vmem(STEPS, rows, cols, depth),
            vmem(3, rows, cols, depth),
            vmem(2, STEPS, cols, depth),
            vmem(2, STEPS, rows, depth),
            vmem(2, STEPS, rows, depth),
            pltpu.VMEM(table, jnp.int32),
            pltpu.VMEM(table, jnp.int32),
            pltpu.SMEM(table, jnp.int32),
            field,
            edges,
            *margins,
            extended,
            bricks,
            field,
            bricks,
            field,
            edges,
            *margins,
            vmem(slots, WIN, LANES, depth),
            vmem(slots, WIN, LANES, depth),
            extended,
            field,
            *margins,
            *margins,
            field,
            bricks,
            bricks,
            *margins,
            *margins,
            vmem(3, rows, cols, depth),
            vmem(BX, BY, depth),
            pltpu.VMEM((slots, depth, depth), jnp.bfloat16),
            pltpu.VMEM((slots, depth, depth), jnp.bfloat16),
            pltpu.SMEM((slots, 12), F32),
            pltpu.SMEM((slots,), jnp.int32),
            pltpu.SMEM((slots,), jnp.int32),
            pltpu.SMEM((slots,), jnp.int32),
            dma((rows // BX,)),
            dma((3,)),
            dma((4,)),
            dma((4,)),
            dma((n_gy,)),
            dma((n_gy,)),
            dma((2, n_gy)),
            dma((2, n_gy)),
            dma((4, 8)),
            dma((4, 8)),
        ],
        compiler_params=pltpu.CompilerParams(
            collective_id=0, has_side_effects=True, vmem_limit_bytes=VMEM_LIMIT
        ),
    )(pulls, owners, codes, states, velocity)


def fold(values, rows_in, cols_in, block, blocks):
    depth = values.shape[2]
    is_first, is_last = block == 0, block == blocks - 1
    rows = cols_in.shape[1] - 16
    zeros = jnp.zeros((8, depth), F32)
    col = lax.broadcasted_iota(jnp.int32, values.shape, 1)
    row = lax.broadcasted_iota(jnp.int32, values.shape, 0)
    values = values + jnp.where(jnp.logical_and(is_last, row == BX - 1), rows_in[0:1], 0.0)
    for i in range(2):
        values = values + jnp.where(
            jnp.logical_and(is_first, row == i), rows_in[1 + i : 2 + i], 0.0
        )
    for side, place in ((0, BY - 1), (1, 0), (2, 1)):
        strip = cols_in[side, pl.ds(8 + block * BX, BX)]
        low = jnp.concatenate([cols_in[side, 0:8], zeros], axis=0)
        high = jnp.concatenate([zeros, cols_in[side, rows + 8 : rows + 16]], axis=0)
        strip = strip + jnp.where(is_first, low, 0.0) + jnp.where(is_last, high, 0.0)
        values = values + jnp.where(col == place, strip[:, None, :], 0.0)
    return values


def body(velocity, states, pull_plan, send_plan, codes):
    _, rows, cols, depth = velocity.shape
    assert cols == BY and rows % BX == 0
    return adjoints_call(
        states,
        velocity,
        pull_plan.reshape(rows // BX),
        send_plan.transpose(0, 1, 3, 2),
        codes.transpose(0, 2, 1),
    )


def solution(mesh):
    return jax.shard_map(
        body,
        mesh=mesh,
        in_specs=(
            P(None, "gx", "gy", None),
            P(None, "gx", "gy", None),
            P("gx", "gy"),
            P("gx", "gy", None, None),
            P(None, "gx", "gy"),
        ),
        out_specs=P(None, "gx", "gy", None),
        check_vma=False,
    )
```

```python
import functools

import jax
import jax.numpy as jnp
from jax import lax
from jax.experimental import pallas as pl
from jax.experimental.pallas import tpu as pltpu
from jax.sharding import PartitionSpec as P

BX = 16
BY = 16
CAP = 2
QF = 8
STEPS = 2
STEP_SIZE = 1.0 / STEPS
WIN = BX + 3
CHUNK = 4
LANES = 24
VMEM_LIMIT = 60 * 1024 * 1024
F32 = jnp.float32


def shape(*dims):
    return jax.ShapeDtypeStruct(dims, F32)


def halo_plan(ins, outs):
    field, cols = ins
    rows_in, cols_in = outs
    rows = field.shape[0]
    main, low, high = pl.ds(8, rows), pl.ds(0, 8), pl.ds(rows + 8, 8)
    first, last = pl.ds(0, 8), pl.ds(rows - 8, 8)
    one, two = pl.ds(0, 1), pl.ds(1, 2)
    remote = [
        (cols.at[one], cols_in.at[one, main], 0, 1),
        (cols.at[two], cols_in.at[two, main], 0, -1),
        (field.at[pl.ds(rows - 1, 1)], rows_in.at[one], 1, 0),
        (field.at[pl.ds(0, 2)], rows_in.at[two], -1, 0),
        (cols.at[one, last], cols_in.at[one, low], 1, 1),
        (cols.at[one, first], cols_in.at[one, high], -1, 1),
        (cols.at[two, last], cols_in.at[two, low], 1, -1),
        (cols.at[two, first], cols_in.at[two, high], -1, -1),
    ]
    return remote


def fold_plan(ins, outs):
    rows_out, cols = ins
    rows_in, cols_in = outs
    rows = cols.shape[1] - 16
    main, low, high = pl.ds(8, rows), pl.ds(0, 8), pl.ds(rows + 8, 8)
    one, two = pl.ds(0, 1), pl.ds(1, 2)
    remote = [
        (cols.at[one, main], cols_in.at[one, main], 0, -1),
        (cols.at[two, main], cols_in.at[two, main], 0, 1),
        (rows_out.at[one], rows_in.at[one], -1, 0),
        (rows_out.at[two], rows_in.at[two], 1, 0),
        (cols.at[one, low], cols_in.at[one, high], -1, -1),
        (cols.at[one, high], cols_in.at[one, low], 1, -1),
        (cols.at[two, low], cols_in.at[two, high], -1, 1),
        (cols.at[two, high], cols_in.at[two, low], 1, 1),
    ]
    return remote


def cubic_weights(f):
    return (
        -f * (f - 1.0) * (f - 2.0) * (1.0 / 6.0),
        (f + 1.0) * (f - 1.0) * (f - 2.0) * 0.5,
        -(f + 1.0) * f * (f - 2.0) * 0.5,
        (f + 1.0) * f * (f - 1.0) * (1.0 / 6.0),
    )


def code_weights(u, v, q):
    depth_shift = lax.shift_right_logical(q, 3)
    fractions = [u, v, jnp.bitwise_and(q, QF - 1)]
    return depth_shift, [cubic_weights(f.astype(F32) * (1.0 / QF)) for f in fractions]


def weighted(weights, terms):
    total = weights[0] * terms[0]
    for weight, term in zip(weights[1:], terms[1:]):
        total = total + weight * term
    return total


def pull_sides(window, weights):
    count = window.shape[0] - 3
    rows = weighted(weights[0], [window[r : r + count] for r in range(4)])
    return weighted(
        weights[1],
        [(rows if t == 0 else pltpu.roll(rows, LANES - t, 1))[:, :BY] for t in range(4)],
    )


def pull_depth(values, shift, weights):
    depth = values.shape[2]
    base = pltpu.roll(values, lax.rem(depth + 1 - shift, depth), 2)
    return weighted(
        weights[2], [base if m == 0 else pltpu.roll(base, depth - m, 2) for m in range(4)]
    )


def push_depth(values, shift, weights):
    depth = values.shape[2]
    base = pltpu.roll(values, lax.rem(depth - 1 + shift, depth), 2)
    return weighted(weights[2], [base if m == 0 else pltpu.roll(base, m, 2) for m in range(4)])


def correlated(w):
    taps = []
    for lag in range(4):
        tap = w[0] * w[lag]
        for m in range(1, 4 - lag):
            tap = tap + w[m] * w[m + lag]
        taps.append(tap)
    return taps


def push_sides(window, values_of, weights):
    carry = None
    for first in range(0, BX, CHUNK):
        values = values_of(first)
        depth = values.shape[2]
        wide = jnp.concatenate([values, jnp.zeros((CHUNK, LANES - BY, depth), F32)], axis=1)
        cols = weighted(weights[1], [wide if t == 0 else pltpu.roll(wide, t, 1) for t in range(4)])
        rows = []
        for i in range(CHUNK + 3):
            terms = [cols[i - r] * weights[0][r] for r in range(4) if 0 <= i - r < CHUNK]
            if carry is not None and i < 3:
                terms.append(carry[i])
            rows.append(sum(terms[1:], terms[0]))
        for i in range(CHUNK):
            window[first + i] = rows[i]
        carry = rows[CHUNK:]
    for i in range(3):
        window[BX + i] = carry[i]


def assemble(extended, field, rows_in, cols_in):
    rows = field.shape[0]
    extended[0:1, 1 : BY + 1, :] = rows_in[0:1]
    extended[rows + 1 : rows + 3, 1 : BY + 1, :] = rows_in[1:3]
    for col, side in ((0, 0), (BY + 1, 1), (BY + 2, 2)):
        extended[:, col, :] = cols_in[side, 7 : rows + 10, :]


def emit_margins(total, acc, rows_out, cols_out):
    rows = total.shape[0]
    rows_out[0:1] = acc[0:1, 1 : BY + 1, :]
    rows_out[1:3] = acc[rows + 1 : rows + 3, 1 : BY + 1, :]
    cols_out[...] = jnp.zeros_like(cols_out)
    for col, side in ((0, 0), (BY + 1, 1), (BY + 2, 2)):
        cols_out[side, 7 : rows + 10, :] = acc[:, col, :]


def gradient(states, rows_in, cols_in, step, block, blocks):
    rows, depth = states.shape[1], states.shape[3]
    first = block * BX
    cells = states[step, pl.ds(first, BX)]
    before = states[step, pl.ds(jnp.maximum(first - 1, 0), 1)]
    after = states[step, pl.ds(jnp.minimum(first + BX, rows - 1), 1)]
    before = jnp.where(block == 0, rows_in[0, pl.ds(step, 1)], before)
    after = jnp.where(block == blocks - 1, rows_in[1, pl.ds(step, 1)], after)
    left = cols_in[0, step, pl.ds(first, BX)][:, None, :]
    right = cols_in[1, step, pl.ds(first, BX)][:, None, :]
    col = lax.broadcasted_iota(jnp.int32, cells.shape, 1)
    below = jnp.concatenate([before, cells[:-1]], axis=0)
    above = jnp.concatenate([cells[1:], after], axis=0)
    lower = jnp.where(col == 0, left, pltpu.roll(cells, 1, 1))
    upper = jnp.where(col == BY - 1, right, pltpu.roll(cells, BY - 1, 1))
    return (
        (above - below) * 0.5,
        (upper - lower) * 0.5,
        (pltpu.roll(cells, depth - 1, 2) - pltpu.roll(cells, 1, 2)) * 0.5,
    )


def adjoints_kernel(
    n_gx, n_gy, pulls, owners, codes, states, velocity,
    force,
    states_v, velocity_v, rows_v, cols_v, edge_cols, request, requested_v, requested_s,
    field, edges, halo_rows, halo_cols, extended, supplied, later_v, inbox,
    next_field, next_edges, next_rows, next_cols, pushed, sums, acc,
    total, late_margin_rows, late_margin_cols, late_fold_rows, late_fold_cols, late,
    outbox, returned, early_margin_rows, early_margin_cols, early_fold_rows, early_fold_cols,
    early_slopes, brick, taps_high, taps_low, kept, rank, order, sorted_owner, save_sem, load_sem, send_sem, recv_sem, code_send, code_recv,
    brick_send, brick_recv, margin_send, margin_recv,
):
    gx, gy = lax.axis_index("gx"), lax.axis_index("gy")
    rows, depth = states.shape[1], states.shape[3]
    blocks, slots = rows // BX, n_gy * CAP

    def pull_of(k):
        return pulls[k]

    def owner_of(slot):
        return owners[0, 0, jnp.bitwise_and(slot, 1), lax.shift_right_logical(slot, 1)]

    def code_of(c, k):
        return codes[c, 0, k]

    def device(step_x, step_y):
        return (lax.rem(gx + step_x + n_gx, n_gx), lax.rem(gy + step_y + n_gy, n_gy))

    def remote(src, dst, send, recv, step_x, step_y):
        return pltpu.make_async_remote_copy(
            src_ref=src, dst_ref=dst, send_sem=send, recv_sem=recv,
            device_id=device(step_x, step_y), device_id_type=pl.DeviceIdType.MESH,
        )

    peers = [(i, j) for i in (-1, 1) for j in (-1, 0, 1)] + [(0, d) for d in range(1, n_gy)]
    barrier = pltpu.get_barrier_semaphore()
    for peer in peers:
        pl.semaphore_signal(
            barrier, inc=1, device_id=device(*peer), device_id_type=pl.DeviceIdType.MESH
        )
    loads = [
        pltpu.make_async_copy(states, states_v, load_sem.at[0]),
        pltpu.make_async_copy(velocity, velocity_v, load_sem.at[1]),
    ]
    for load in loads:
        load.start()
    peer_row = lax.broadcasted_iota(jnp.int32, request.shape, 0)
    entry = lax.broadcasted_iota(jnp.int32, request.shape, 1)
    lane = lax.broadcasted_iota(jnp.int32, request.shape, 2)
    place = jnp.where(entry < CAP, peer_row * CAP + entry, -1)
    table = jnp.zeros(request.shape, jnp.int32)
    for k in range(blocks):
        triple = jnp.where(
            lane == 0, code_of(0, k), jnp.where(lane == 1, code_of(1, k), code_of(2, k))
        )
        table = jnp.where(place == pull_of(k), triple, table)
    request[...] = table
    requested_v[pl.ds(gy, 1)] = request[pl.ds(gy, 1)]
    loads[0].wait()
    for step in range(STEPS):
        edge_cols[0, step] = states_v[step, :, BY - 1, :]
        edge_cols[1, step] = states_v[step, :, 0, :]
    pl.semaphore_wait(barrier, len(peers))

    copies = [
        remote(edge_cols.at[0], cols_v.at[0], send_sem.at[0], recv_sem.at[0], 0, 1),
        remote(edge_cols.at[1], cols_v.at[1], send_sem.at[1], recv_sem.at[1], 0, -1),
        remote(states_v.at[:, rows - 1], rows_v.at[0], send_sem.at[2], recv_sem.at[2], 1, 0),
        remote(states_v.at[:, 0], rows_v.at[1], send_sem.at[3], recv_sem.at[3], -1, 0),
    ]
    for copy in copies:
        copy.start()
    code_copies = []
    for d in range(1, n_gy):
        peer = lax.rem(gy + d, n_gy)
        code_copies.append(
            remote(request.at[peer], requested_v.at[gy], code_send.at[d], code_recv.at[d], 0, d)
        )
    for copy in code_copies:
        copy.start()
    loads[1].wait()
    for copy in copies:
        copy.wait()

    @pl.loop(0, blocks)
    def _(block):
        cells = pl.ds(block * BX, BX)
        terms = []
        for step in range(STEPS):
            parts = gradient(states_v, rows_v, cols_v, step, block, blocks)
            terms.append(
                (
                    velocity_v[0, cells] * parts[0]
                    + velocity_v[1, cells] * parts[1]
                    + velocity_v[2, cells] * parts[2]
                )
                * -STEP_SIZE
            )
        field[cells] = terms[0]
        for side, col in ((0, BY - 1), (1, 0), (2, 1)):
            edges[side, cells] = terms[0][:, col, :]
        later_v[cells] = terms[1]

    def margin_copies(phase, moves):
        copies = [
            remote(src, dst, margin_send.at[phase, i], margin_recv.at[phase, i], step_x, step_y)
            for i, (src, dst, step_x, step_y) in enumerate(moves)
        ]
        for copy in copies:
            copy.start()
        return copies

    copies = margin_copies(0, halo_plan((field, edges), (halo_rows, halo_cols)))
    for copy in code_copies:
        copy.wait()
    table_copy = pltpu.make_async_copy(requested_v, requested_s, load_sem.at[2])
    table_copy.start()
    table_copy.wait()
    extended[1 : rows + 1, 1 : BY + 1, :] = field[...]
    for copy in copies:
        copy.wait()
    assemble(extended, field, halo_rows, halo_cols)

    def codes_of(slot):
        peer, e = lax.shift_right_logical(slot, 1), jnp.bitwise_and(slot, 1)
        return code_weights(*[requested_s[peer, e, c] for c in range(3)])

    def supply(peer, target):
        for e in range(CAP):
            slot = peer * CAP + e
            first = jnp.maximum(owner_of(slot), 0) * BX
            shift, weights = codes_of(slot)
            for row in range(0, BX, CHUNK):
                sides = pull_sides(extended[pl.ds(first + row, CHUNK + 3)], weights)
                target[slot, row : row + CHUNK] = pull_depth(sides, shift, weights)

    def brick_copy(phase, d, source, target):
        peer = lax.rem(gy + d, n_gy)
        return remote(
            source.at[pl.ds(peer * CAP, CAP)], target.at[pl.ds(gy * CAP, CAP)],
            brick_send.at[phase, d], brick_recv.at[phase, d], 0, d,
        )

    @pl.loop(1, n_gy)
    def _(d):
        supply(lax.rem(gy + d, n_gy), supplied)
        brick_copy(0, d, supplied, inbox).start()

    supply(gy, inbox)

    @pl.loop(0, slots)
    def _(s):
        _, weights = codes_of(s)
        for axis in range(3):
            for m in range(4):
                kept[s, 4 * axis + m] = weights[axis][m]
        taps = correlated(weights[2])
        row = lax.broadcasted_iota(jnp.int32, (depth, depth), 0)
        col = lax.broadcasted_iota(jnp.int32, (depth, depth), 1)
        gap = jnp.abs(row - col)
        gap = jnp.minimum(gap, depth - gap)
        matrix = jnp.zeros((depth, depth), F32)
        for lag in range(4):
            matrix = jnp.where(gap == lag, taps[lag], matrix)
        high = matrix.astype(jnp.bfloat16)
        taps_high[s] = high
        taps_low[s] = (matrix - high.astype(F32)).astype(jnp.bfloat16)

    def kept_weights(slot):
        return [[kept[slot, 4 * axis + m] for m in range(4)] for axis in range(3)]

    def correlate(slot, values):
        high = values.astype(jnp.bfloat16)
        low = (values - high.astype(F32)).astype(jnp.bfloat16)

        def dot(left, right):
            return jnp.dot(left, right, preferred_element_type=F32)

        return (
            dot(high, taps_low[slot]) + dot(low, taps_high[slot]) + dot(high, taps_high[slot])
        )

    @pl.loop(0, slots)
    def _(s):
        mine = owner_of(s)

        def ahead(t, count):
            other = owner_of(t)
            before = jnp.logical_or(other < mine, jnp.logical_and(other == mine, t < s))
            return count + jnp.where(before, 1, 0)

        rank[s] = lax.fori_loop(0, slots, ahead, 0)

    @pl.loop(0, slots)
    def _(j):
        found = lax.fori_loop(0, slots, lambda t, at: jnp.where(rank[t] == j, t, at), 0)
        order[j] = found
        sorted_owner[j] = owner_of(found)

    @pl.loop(1, n_gy)
    def _(d):
        brick_copy(0, d, supplied, inbox).wait()

    @pl.loop(0, blocks)
    def _(block):
        cells = pl.ds(block * BX, BX)
        values = inbox[pull_of(block)] + later_v[cells]
        next_field[cells] = values
        for side, col in ((0, BY - 1), (1, 0), (2, 1)):
            next_edges[side, cells] = values[:, col, :]

    copies = margin_copies(1, halo_plan((next_field, next_edges), (next_rows, next_cols)))
    extended[1 : rows + 1, 1 : BY + 1, :] = next_field[...]
    for copy in copies:
        copy.wait()
    assemble(extended, next_field, next_rows, next_cols)

    def accumulate():
        sums[0] = jnp.zeros(sums.shape[1:], F32)

        @pl.loop(0, slots)
        def _(j):
            before = jnp.maximum(j - 1, 0)
            same = sorted_owner[j] == sorted_owner[before]
            sums[j] = jnp.where(same, sums[before], 0.0) + pushed[order[j]]

        acc[...] = jnp.zeros_like(acc)

        @pl.loop(0, blocks)
        def _(k):
            def at_most(t, count):
                return count + jnp.where(sorted_owner[t] <= k, 1, 0)

            last = jnp.maximum(lax.fori_loop(0, slots, at_most, 0) - 1, 0)
            window = pl.ds(k * BX, WIN)
            acc[window] = acc[window] + jnp.where(sorted_owner[last] == k, sums[last], 0.0)

    def fold_all(fold_rows, fold_cols, target):
        @pl.loop(0, blocks)
        def _(block):
            cells = pl.ds(block * BX, BX)
            target[cells] = fold(total[cells], fold_rows, fold_cols, block, blocks)

    @pl.loop(0, slots)
    def _(slot):
        first = jnp.maximum(owner_of(slot), 0) * BX
        weights = kept_weights(slot)
        for row in range(0, BX, CHUNK):
            brick[row : row + CHUNK] = pull_sides(
                extended[pl.ds(first + row, CHUNK + 3)], weights
            )
        values = correlate(slot, brick[...].reshape(BX * BY, depth))
        brick[...] = values.reshape(BX, BY, depth)
        push_sides(pushed.at[slot], lambda row: brick[row : row + CHUNK], weights)

    accumulate()
    emit_margins(total, acc, late_margin_rows, late_margin_cols)
    moves = fold_plan((late_margin_rows, late_margin_cols), (late_fold_rows, late_fold_cols))
    copies = margin_copies(2, moves)
    total[...] = acc[1 : rows + 1, 1 : BY + 1, :]
    for copy in copies:
        copy.wait()
    fold_all(late_fold_rows, late_fold_cols, late)
    def fill(peer, target):
        for e in range(CAP):
            slot = peer * CAP + e
            source = 0
            for k in range(1, blocks):
                source = jnp.where(pull_of(k) == slot, k, source)
            target[slot] = late[pl.ds(source * BX, BX)]

    @pl.loop(1, n_gy)
    def _(d):
        fill(lax.rem(gy + d, n_gy), outbox)
        brick_copy(1, d, outbox, returned).start()

    fill(gy, returned)

    @pl.loop(0, blocks)
    def _(block):
        cells = pl.ds(block * BX, BX)
        scaled = late[cells] * -STEP_SIZE
        parts = gradient(states_v, rows_v, cols_v, 1, block, blocks)
        slopes = gradient(states_v, rows_v, cols_v, 0, block, blocks)
        for c in range(3):
            velocity_v[c, cells] = scaled * parts[c]
            early_slopes[c, cells] = slopes[c]

    def push(peer):
        for e in range(CAP):
            slot = peer * CAP + e
            peer_row, e_row = lax.shift_right_logical(slot, 1), jnp.bitwise_and(slot, 1)
            shift = lax.shift_right_logical(requested_s[peer_row, e_row, 2], 3)
            weights = kept_weights(slot)
            push_sides(
                pushed.at[slot],
                lambda row: push_depth(returned[slot, row : row + CHUNK], shift, weights),
                weights,
            )

    push(gy)

    @pl.loop(1, n_gy)
    def _(d):
        brick_copy(1, d, outbox, returned).wait()
        push(lax.rem(gy + n_gy - d, n_gy))

    accumulate()
    emit_margins(total, acc, early_margin_rows, early_margin_cols)
    moves = fold_plan((early_margin_rows, early_margin_cols), (early_fold_rows, early_fold_cols))
    copies = margin_copies(3, moves)
    total[...] = acc[1 : rows + 1, 1 : BY + 1, :]
    for copy in copies:
        copy.wait()

    def save(block):
        cells = pl.ds(block * BX, BX)
        return pltpu.make_async_copy(
            velocity_v.at[:, cells], force.at[:, cells], save_sem.at[block]
        )

    @pl.loop(0, blocks)
    def _(block):
        cells = pl.ds(block * BX, BX)
        early = fold(total[cells], early_fold_rows, early_fold_cols, block, blocks)
        scaled = early * -STEP_SIZE
        for c in range(3):
            velocity_v[c, cells] = velocity_v[c, cells] + scaled * early_slopes[c, cells]
        save(block).start()

    @pl.loop(0, blocks)
    def _(block):
        save(block).wait()


def adjoints_call(states, velocity, pulls, owners, codes):
    n_gx, n_gy = lax.axis_size("gx"), lax.axis_size("gy")
    _, rows, cols, depth = states.shape
    slots = n_gy * CAP
    table = (n_gy, 8, 128)
    hbm = pl.BlockSpec(memory_space=pltpu.HBM)
    dma = pltpu.SemaphoreType.DMA

    def vmem(*dims):
        return pltpu.VMEM(dims, F32)

    field = vmem(rows, cols, depth)
    edges = vmem(3, rows, depth)
    margin_rows, margin_cols = vmem(3, cols, depth), vmem(3, rows + 16, depth)
    extended = vmem(rows + 3, LANES, depth)
    bricks = vmem(slots, BX, BY, depth)
    margins = [margin_rows, margin_cols]
    return pl.pallas_call(
        lambda *refs: adjoints_kernel(n_gx, n_gy, *refs),
        name="adjoints",
        in_specs=[pl.BlockSpec(memory_space=pltpu.SMEM)] * 3 + [hbm, hbm],
        out_specs=hbm,
        out_shape=shape(3, rows, cols, depth),
        scratch_shapes=[
            vmem(STEPS, rows, cols, depth),
            vmem(3, rows, cols, depth),
            vmem(2, STEPS, cols, depth),
            vmem(2, STEPS, rows, depth),
            vmem(2, STEPS, rows, depth),
            pltpu.VMEM(table, jnp.int32),
            pltpu.VMEM(table, jnp.int32),
            pltpu.SMEM(table, jnp.int32),
            field,
            edges,
            *margins,
            extended,
            bricks,
            field,
            bricks,
            field,
            edges,
            *margins,
            vmem(slots, WIN, LANES, depth),
            vmem(slots, WIN, LANES, depth),
            extended,
            field,
            *margins,
            *margins,
            field,
            bricks,
            bricks,
            *margins,
            *margins,
            vmem(3, rows, cols, depth),
            vmem(BX, BY, depth),
            pltpu.VMEM((slots, depth, depth), jnp.bfloat16),
            pltpu.VMEM((slots, depth, depth), jnp.bfloat16),
            pltpu.SMEM((slots, 12), F32),
            pltpu.SMEM((slots,), jnp.int32),
            pltpu.SMEM((slots,), jnp.int32),
            pltpu.SMEM((slots,), jnp.int32),
            dma((rows // BX,)),
            dma((3,)),
            dma((4,)),
            dma((4,)),
            dma((n_gy,)),
            dma((n_gy,)),
            dma((2, n_gy)),
            dma((2, n_gy)),
            dma((4, 8)),
            dma((4, 8)),
        ],
        compiler_params=pltpu.CompilerParams(
            collective_id=0, has_side_effects=True, vmem_limit_bytes=VMEM_LIMIT
        ),
    )(pulls, owners, codes, states, velocity)


def fold(values, rows_in, cols_in, block, blocks):
    depth = values.shape[2]
    is_first, is_last = block == 0, block == blocks - 1
    rows = cols_in.shape[1] - 16
    zeros = jnp.zeros((8, depth), F32)
    col = lax.broadcasted_iota(jnp.int32, values.shape, 1)
    row = lax.broadcasted_iota(jnp.int32, values.shape, 0)
    values = values + jnp.where(jnp.logical_and(is_last, row == BX - 1), rows_in[0:1], 0.0)
    for i in range(2):
        values = values + jnp.where(
            jnp.logical_and(is_first, row == i), rows_in[1 + i : 2 + i], 0.0
        )
    for side, place in ((0, BY - 1), (1, 0), (2, 1)):
        strip = cols_in[side, pl.ds(8 + block * BX, BX)]
        low = jnp.concatenate([cols_in[side, 0:8], zeros], axis=0)
        high = jnp.concatenate([zeros, cols_in[side, rows + 8 : rows + 16]], axis=0)
        strip = strip + jnp.where(is_first, low, 0.0) + jnp.where(is_last, high, 0.0)
        values = values + jnp.where(col == place, strip[:, None, :], 0.0)
    return values


def body(velocity, states, pull_plan, send_plan, codes):
    _, rows, cols, depth = velocity.shape
    assert cols == BY and rows % BX == 0
    return adjoints_call(
        states,
        velocity,
        pull_plan.reshape(rows // BX),
        send_plan.transpose(0, 1, 3, 2),
        codes.transpose(0, 2, 1),
    )


def solution(mesh):
    return jax.shard_map(
        body,
        mesh=mesh,
        in_specs=(
            P(None, "gx", "gy", None),
            P(None, "gx", "gy", None),
            P("gx", "gy"),
            P("gx", "gy", None, None),
            P(None, "gx", "gy"),
        ),
        out_specs=P(None, "gx", "gy", None),
        check_vma=False,
    )
```
